256 devices in a mesh: lines: 64 (over z, y, core), seg: 4 (over x).
Axes of the slice: x: 4, y: 4, z: 8, core: 2. Of those that a mesh axis runs over, the one named last changes fastest.
Arguments:
- diag_blocks: float32 [128, 16, 4096], P('lines', 'seg'), may hold values from -0.0021 to 0.0221, as said below
- couplings: float32 [128, 16, 4096], P('lines', 'seg'), may hold values from -0.363 to 1.363
- cross_weight: float32 [128, 1024], P('lines', 'seg'), may hold values from 0.001 to 0.0033
- right_side: float32 [128, 1024], P('lines', 'seg'), may hold values from -2.4 to 2.4
Outputs:
- solution_field: float32 [128, 1024], P('lines', 'seg')
- residual: float32 [128, 1024], P('lines', 'seg')
The draws below stay inside these ranges and needn't reach their ends.
Inputs may be any that keep to these rules, and one draw needn't show every extreme that they name: Every block of diag_blocks is symmetric positive definite, every block of couplings is symmetric positive semidefinite, and the operator A is symmetric positive definite.
All inputs are finite; a program needn't handle non-finite values.
Results may differ from the reference program's by a relative error of at most 0.00065.
Values sent between devices are 32-bit elements; how exact they have to be, the bound alone decides.
A program may use at most 64 MiB of HBM per device.

```python
import math
import jax
import jax.numpy as jnp
from jax import lax

BLOCK = 64
ITERS = 4
LINES = 128
ELEMS = 16


def permuted_part(key, amplitude):
    scores = jax.random.randint(key, (LINES, ELEMS, BLOCK), 0, 4096) * BLOCK + jnp.arange(BLOCK, dtype=jnp.int32)
    ranking = jnp.argsort(scores, axis=-1)
    placed = (ranking[..., :, None] == jnp.arange(BLOCK, dtype=jnp.int32)).astype(jnp.float32)
    spread = placed * amplitude[..., :, None]
    return 0.5 * (spread + jnp.swapaxes(spread, -1, -2))


def symmetric_noise(key, bound):
    raw_noise = jax.random.uniform(key, (LINES, ELEMS, BLOCK, BLOCK), jnp.float32, -bound, bound)
    return 0.5 * (raw_noise + jnp.swapaxes(raw_noise, -1, -2))


def assemble(diagonal_values, permuted, noise):
    identity = jnp.eye(BLOCK, dtype=jnp.float32)
    blocks = identity * diagonal_values[..., :, None] + permuted + noise
    return blocks.reshape(LINES, ELEMS, BLOCK * BLOCK)


def draw_diag_blocks(key, part):
    key = jax.random.fold_in(key, 11)
    first_key, second_key, third_key, fourth_key = jax.random.split(key, 4)
    shape = (LINES, ELEMS, BLOCK)
    diagonal_values = jnp.exp(jax.random.uniform(first_key, shape, jnp.float32, math.log(0.01), math.log(0.02)))
    amplitude = jax.random.uniform(second_key, shape, jnp.float32, -0.002, 0.002)
    return assemble(diagonal_values, permuted_part(third_key, amplitude), symmetric_noise(fourth_key, 2e-05))


def draw_couplings(key, part):
    key = jax.random.fold_in(key, 17)
    first_key, second_key, third_key, fourth_key = jax.random.split(key, 4)
    shape = (LINES, ELEMS, BLOCK)
    diagonal_values = jnp.exp(jax.random.uniform(first_key, shape, jnp.float32, math.log(0.5), math.log(1.0)))
    amplitude = jax.random.uniform(second_key, shape, jnp.float32, -0.36, 0.36)
    return assemble(diagonal_values, permuted_part(third_key, amplitude), symmetric_noise(fourth_key, 0.002))


def draw_right_side(key, part):
    key = jax.random.fold_in(key, 23)
    line_pos = jnp.arange(LINES, dtype=jnp.float32) / max(LINES - 1, 1)
    elem_pos = (jnp.arange(ELEMS * BLOCK) // BLOCK).astype(jnp.float32) / max(ELEMS - 1, 1)
    row_scale = (1.0 + 2.0 * line_pos)[:, None] * (1.0 + 2.0 * elem_pos)[None, :] / 3.0
    entries = jnp.clip(jax.random.normal(key, (LINES, ELEMS * BLOCK), jnp.float32), -4.0, 4.0)
    return 0.2 * entries * row_scale


def level_of(stream_key, dims, cuts, least, largest):
    loudness = 1.0
    for position, shards_of in cuts:
        draws = jax.random.uniform(jax.random.fold_in(jax.random.fold_in(stream_key, 6), position), (shards_of,), jnp.float32, least / len(cuts), largest / len(cuts))
        loudness = loudness * jnp.repeat(jnp.exp(draws), dims[position] // shards_of).reshape((-1,) + (1,) * (len(dims) - 1 - position))
    return loudness


def setup_inputs(seed: int = 0) -> dict:
    keys = jax.random.split(jax.random.key(seed), 5)
    diag_blocks = draw_diag_blocks(jax.random.fold_in(keys[4], 71), 0)
    couplings = draw_couplings(jax.random.fold_in(keys[4], 71), 0)
    cross_weight = jnp.clip(jnp.exp(math.log(0.0033) - 1.1939224 * jax.random.uniform(keys[2], (LINES, ELEMS * BLOCK), jnp.float32) ** level_of(keys[2], (LINES, ELEMS * BLOCK), ((0, 64), (1, 4)), -0.2, 0.2)), 0.001, 0.0033)
    right_side = draw_right_side(jax.random.fold_in(keys[4], 71), 0)
    return dict(diag_blocks=diag_blocks, couplings=couplings, cross_weight=cross_weight, right_side=right_side)


precise = lax.Precision.HIGHEST

def spd_inverse(matrix):
    lower_factor = jnp.linalg.cholesky(matrix)
    identity = jnp.broadcast_to(jnp.eye(matrix.shape[-1], dtype=matrix.dtype), matrix.shape)
    lower_inv = jax.scipy.linalg.solve_triangular(lower_factor, identity, lower=True)
    return jnp.einsum('...ki,...kj->...ij', lower_inv, lower_inv, precision=precise)

def block_factor(diag_seq, link_seq):
    zero_block = jnp.zeros_like(diag_seq[:1])
    link_before = jnp.concatenate([zero_block, link_seq], axis=0)
    link_after = jnp.concatenate([link_seq, zero_block], axis=0)

    def advance(carry_link, pieces):
        diag_now, before_now, after_now = pieces
        schur_block = diag_now - jnp.einsum('lji,ljk->lik', before_now, carry_link, precision=precise)
        inverse = spd_inverse(schur_block)
        coupled = jnp.einsum('lij,ljk->lik', inverse, after_now, precision=precise)
        return (coupled, (inverse, coupled))
    last_coupled, outputs = lax.scan(advance, zero_block[0], (diag_seq, link_before, link_after))
    return outputs

def block_solve(inverses, coupled, rhs_seq):
    coupled_before = jnp.concatenate([jnp.zeros_like(coupled[:1]), coupled[:-1]], axis=0)

    def forward(prev_value, pieces):
        link_now, rhs_now = pieces
        current = rhs_now - jnp.einsum('lji,lj...->li...', link_now, prev_value, precision=precise)
        return (current, current)
    last_forward, reduced = lax.scan(forward, jnp.zeros_like(rhs_seq[0]), (coupled_before, rhs_seq))

    def backward(next_value, pieces):
        inverse, link_now, reduced_now = pieces
        current = jnp.einsum('lij,lj...->li...', inverse, reduced_now, precision=precise)
        current = current - jnp.einsum('lij,lj...->li...', link_now, next_value, precision=precise)
        return (current, current)
    last_backward, result = lax.scan(backward, jnp.zeros_like(rhs_seq[0]), (inverses, coupled, reduced), reverse=True)
    return result

def reference(diag_blocks, couplings, cross_weight, right_side):

    def to_sequence(vector):
        return vector.reshape(LINES, ELEMS, BLOCK).transpose(1, 0, 2)

    def from_sequence(sequence):
        return sequence.transpose(1, 0, 2).reshape(LINES, ELEMS * BLOCK)
    mass_seq = diag_blocks.reshape(LINES, ELEMS, BLOCK, BLOCK).transpose(1, 0, 2, 3)
    edge_full = couplings.reshape(LINES, ELEMS, BLOCK, BLOCK).transpose(1, 0, 2, 3)
    edge_prior = jnp.concatenate([jnp.zeros_like(edge_full[:1]), edge_full[:-1]], axis=0)
    diag_seq = mass_seq + edge_full + edge_prior
    link_full = -edge_full
    inverses, coupled = block_factor(diag_seq, link_full[:-1])
    link_used = jnp.concatenate([link_full[:-1], jnp.zeros_like(link_full[:1])], axis=0)
    link_prior = jnp.concatenate([jnp.zeros_like(link_full[:1]), link_used[:-1]], axis=0)

    def operate(field):
        sequence = to_sequence(field)
        zero_row = jnp.zeros_like(sequence[:1])
        after_vals = jnp.concatenate([sequence[1:], zero_row], axis=0)
        before_vals = jnp.concatenate([zero_row, sequence[:-1]], axis=0)
        line_part = jnp.einsum('elij,elj->eli', diag_seq, sequence, precision=precise)
        line_part = line_part + jnp.einsum('elij,elj->eli', link_used, after_vals, precision=precise)
        line_part = line_part + jnp.einsum('elji,elj->eli', link_prior, before_vals, precision=precise)
        across = cross_weight * jnp.roll(field, -1, 0) + jnp.roll(cross_weight, 1, 0) * jnp.roll(field, 1, 0)
        return from_sequence(line_part) - across

    def precondition(vector):
        return from_sequence(block_solve(inverses, coupled, to_sequence(vector)))
    solution_field = jnp.zeros_like(right_side)
    residual = right_side
    search = precondition(residual)
    direction = search
    energy = jnp.sum(residual * search)
    for sweep_turn in range(ITERS):
        image = operate(direction)
        step_size = energy / jnp.sum(direction * image)
        solution_field = solution_field + step_size * direction
        residual = residual - step_size * image
        if sweep_turn + 1 < ITERS:
            search = precondition(residual)
            new_energy = jnp.sum(residual * search)
            direction = search + new_energy / energy * direction
            energy = new_energy
    return (solution_field, residual)
```

```python
import functools

import jax
import jax.numpy as jnp
from jax import lax
from jax.experimental import pallas as pl
from jax.experimental.pallas import tpu as pltpu
from jax.sharding import PartitionSpec as P

B = 64
F32 = jnp.float32
MESH = pl.DeviceIdType.MESH
VMEM = pl.BlockSpec(memory_space=pltpu.VMEM)
EXACT = lax.Precision.HIGHEST


def mm(a, b):
    return jnp.dot(a, b, precision=EXACT, preferred_element_type=F32)


def mm_nt(a, b):
    return lax.dot_general(a, b, (((1,), (1,)), ((), ())), precision=EXACT, preferred_element_type=F32)


def invert(work, packs):
    lane = lax.broadcasted_iota(jnp.int32, (8, 2 * B), 1)
    half = jnp.where(lane < B, 0, B)
    inner = lane - half

    def step(i, carry):
        k = 2 * i
        at0, at1 = half + k, half + k + 1
        is0, is1 = inner == k, inner == k + 1
        both = jnp.logical_or(is0, is1)
        for p in range(packs):
            r0 = jnp.broadcast_to(work[pl.ds(B * p + k, 1), :], (8, 2 * B))
            r1 = jnp.broadcast_to(work[pl.ds(B * p + k + 1, 1), :], (8, 2 * B))
            a = jnp.take_along_axis(r0, at0, axis=1, mode="promise_in_bounds")
            b = jnp.take_along_axis(r0, at1, axis=1, mode="promise_in_bounds")
            d = jnp.take_along_axis(r1, at1, axis=1, mode="promise_in_bounds")
            inv = 1.0 / (a * d - b * b)
            ai, bi, di = a * inv, b * inv, d * inv
            n0 = jnp.where(is0, di, jnp.where(is1, -bi, di * r0 - bi * r1))
            n1 = jnp.where(is0, -bi, jnp.where(is1, ai, ai * r1 - bi * r0))
            for t in range(B // 8):
                rows = pl.ds(B * p + 8 * t, 8)
                tile = work[rows, :]
                c0 = jnp.take_along_axis(tile, at0, axis=1, mode="promise_in_bounds")
                c1 = jnp.take_along_axis(tile, at1, axis=1, mode="promise_in_bounds")
                work[rows, :] = jnp.where(both, 0.0, tile) - c0 * n0 - c1 * n1
            work[pl.ds(B * p + k, 1), :] = n0[:1]
            work[pl.ds(B * p + k + 1, 1), :] = n1[:1]
        return carry

    lax.fori_loop(0, B // 2, step, 0)


def interior_kernel(diag, coup, gz, hh, xyz, dmat, pmat, work):
    lines = diag.shape[0]
    last = lax.axis_index("seg") == lax.axis_size("seg") - 1
    not_first = lax.broadcasted_iota(jnp.int32, (4, 2 * B), 0) > 0
    for l in range(lines):
        for k in range(B * B // (2 * B)):
            cols = pl.ds(2 * B * k, 2 * B)
            edge = coup[l, :, cols]
            before = jnp.concatenate([edge[3:], edge[:3]], axis=0)
            full = diag[l, :, cols] + edge + jnp.where(not_first, before, 0.0)
            for dst, tile in ((dmat, full), (pmat, edge)):
                dst[pl.ds(4 * B * l + 2 * k, 4, stride=B), :] = tile
                dst[pl.ds(4 * B * l + 2 * k + 1, 4, stride=B), :] = jnp.concatenate([tile[:, B:], tile[:, :B]], axis=1)

    def d_of(l, e):
        return dmat[pl.ds(4 * B * l + B * e, B), :B]

    def p_of(l, e):
        return pmat[pl.ds(4 * B * l + B * e, B), :B]

    for l in range(lines):
        work[pl.ds(B * l, B), :] = jnp.concatenate([d_of(l, 1), d_of(l, 3)], axis=1)
    invert(work, lines)
    i1 = [work[pl.ds(B * l, B), :B] for l in range(lines)]
    i3 = [work[pl.ds(B * l, B), B:] for l in range(lines)]
    u1 = [mm(i1[l], p_of(l, 1)) for l in range(lines)]
    u3 = [mm(i3[l], p_of(l, 2)) for l in range(lines)]
    s2 = [d_of(l, 2) - mm(p_of(l, 1), u1[l]) - mm(p_of(l, 2), u3[l]) for l in range(lines)]
    work[pl.ds(0, B), :] = jnp.concatenate(s2, axis=1)
    invert(work, 1)
    eye = (
        lax.broadcasted_iota(jnp.int32, (B, 2 * B), 0) == lax.broadcasted_iota(jnp.int32, (B, 2 * B), 1)
    ).astype(F32)
    zero = jnp.zeros((B, B), F32)
    for l in range(lines):
        i2 = work[pl.ds(0, B), B * l : B * l + B]
        w1, w3 = mm(u1[l], i2), mm(u3[l], i2)
        g21, g23 = mm_nt(i2, u1[l]), mm_nt(i2, u3[l])
        g11, g13 = i1[l] + mm_nt(w1, u1[l]), mm_nt(w1, u3[l])
        g31, g33 = mm_nt(w3, u1[l]), i3[l] + mm_nt(w3, u3[l])
        gz[l, 0:B, :] = jnp.zeros((B, 4 * B), F32)
        gz[l, B : 2 * B, :] = jnp.concatenate([zero, g11, w1, g13], axis=1)
        gz[l, 2 * B : 3 * B, :] = jnp.concatenate([zero, g21, i2, g23], axis=1)
        gz[l, 3 * B :, :] = jnp.concatenate([zero, g31, w3, g33], axis=1)
        p0 = p_of(l, 0)
        p3 = jnp.where(last, 0.0, p_of(l, 3))
        h1 = mm(jnp.concatenate([g11, g21, g31], axis=0), p0)
        h3 = mm(jnp.concatenate([g13, g23, g33], axis=0), p3)
        hh[l, 0:B, :] = eye
        hh[l, B:, :] = jnp.concatenate([h1, h3], axis=1)
        x = d_of(l, 0) - mm(p0, h1[:B])
        y = p3 - mm(p3, h3[2 * B :])
        xyz[l, :, :] = jnp.concatenate([x, y], axis=1)
        xyz[lines, :, B * l : B * l + B] = mm(p0, h3[:B])


def meet(peers):
    barrier = pltpu.get_barrier_semaphore()
    for peer in peers:
        pl.semaphore_signal(barrier, inc=1, device_id=peer, device_id_type=MESH)
    pl.semaphore_wait(barrier, len(peers))


def gather_kernel(mine, out, slots, send_sem, recv_sem):
    line, me = lax.axis_index("lines"), lax.axis_index("seg")
    count = slots.shape[0]
    others = [lax.rem(me + d, count) for d in range(1, count)]
    meet([(line, other) for other in others])
    sends = []
    for d, other in enumerate(others):
        copy = pltpu.make_async_remote_copy(
            src_ref=mine,
            dst_ref=slots.at[me],
            send_sem=send_sem.at[d],
            recv_sem=recv_sem.at[me],
            device_id=(line, other),
            device_id_type=MESH,
        )
        copy.start()
        sends.append(copy)
    out[me] = mine[...]
    for d, other in enumerate(others):
        pltpu.make_async_remote_copy(
            src_ref=mine,
            dst_ref=slots.at[other],
            send_sem=send_sem.at[d],
            recv_sem=recv_sem.at[other],
            device_id=(line, other),
            device_id_type=MESH,
        ).wait_recv()
        out[other] = slots[other]
    for copy in sends:
        copy.wait_send()


def reduced_kernel(xyz, hh, post, work, sigma):
    lines = hh.shape[0]
    me = lax.axis_index("seg")

    def diag_of(l, s):
        block = xyz[s, l, :, :B]
        return block if s == 0 else block + xyz[s - 1, l, :, B:]

    def z_of(l, s):
        return xyz[s, lines, :, B * l : B * l + B]

    for l in range(lines):
        work[pl.ds(B * l, B), :] = jnp.concatenate([diag_of(l, 0), diag_of(l, 3)], axis=1)
    invert(work, lines)
    every = range(lines)
    j0 = [work[pl.ds(B * l, B), :B] for l in every]
    j3 = [work[pl.ds(B * l, B), B:] for l in every]
    v0 = [mm(j0[l], z_of(l, 0)) for l in every]
    v3 = [mm_nt(j3[l], z_of(l, 2)) for l in every]
    s11 = [diag_of(l, 1) - mm(z_of(l, 0).T, v0[l]) for l in every]
    s22 = [diag_of(l, 2) - mm(z_of(l, 2), v3[l]) for l in every]
    work[pl.ds(0, B), :] = jnp.concatenate(s11, axis=1)
    invert(work, 1)
    j1 = [work[pl.ds(0, B), B * l : B * l + B] for l in every]
    v1 = [mm(j1[l], z_of(l, 1)) for l in every]
    s22 = [s22[l] - mm(z_of(l, 1).T, v1[l]) for l in every]
    work[pl.ds(0, B), :] = jnp.concatenate(s22, axis=1)
    invert(work, 1)
    for l in every:
        e22 = work[pl.ds(0, B), B * l : B * l + B]
        e12, e21 = mm(v1[l], e22), mm_nt(e22, v1[l])
        e11 = j1[l] + mm_nt(e12, v1[l])
        e01, e02 = mm(v0[l], e11), mm(v0[l], e12)
        e10, e20 = mm_nt(e11, v0[l]), mm_nt(e21, v0[l])
        e31, e32 = mm(v3[l], e21), mm(v3[l], e22)
        e13, e23 = mm_nt(e12, v3[l]), mm_nt(e22, v3[l])
        e00 = j0[l] + mm_nt(e01, v0[l])
        e33 = j3[l] + mm_nt(e32, v3[l])
        e03, e30 = mm_nt(e02, v3[l]), mm(v3[l], e20)
        for s, row in enumerate(((e00, e01, e02, e03), (e10, e11, e12, e13), (e20, e21, e22, e23), (e30, e31, e32, e33))):
            sigma[pl.ds(B * s, B), :] = jnp.concatenate(row, axis=1)
        sigma[pl.ds(4 * B, B), :] = jnp.zeros((B, 4 * B), F32)
        rows = sigma[pl.ds(pl.multiple_of(B * me, B), 2 * B), :]
        post[l] = mm(hh[l], rows).T


def solve_kernel(
    dims, gz, hh, post, weight, right, out_x, out_r,
    edge, edge_in, sep, sep_in, sums, sums_in, edge_send, edge_recv, sep_send, sep_recv, sum_send, sum_recv,
):
    nl, ns, ny = dims
    line, me = lax.axis_index("lines"), lax.axis_index("seg")
    left, right_of = lax.rem(line + nl - 1, nl), lax.rem(line + 1, nl)
    core, y_at, z_at = lax.rem(line, 2), lax.rem(line // 2, ny), line // (2 * ny)
    nz = nl // (2 * ny)

    def near(index):
        return ((z_at * ny + index // ns) * 2 + core, lax.rem(index, ns))

    def far(index):
        return (((index // 2) * ny + y_at) * 2 + lax.rem(index, 2), me)

    groups = ((near, ns * ny, y_at * ns + me), (far, 2 * nz, z_at * 2 + core))
    peers = [(left, me), (right_of, me)] + [(line, lax.rem(me + d, ns)) for d in range(1, ns)]
    for place, size, own in groups:
        peers += [place(lax.rem(own + d, size)) for d in range(1, size)]
    meet(peers)
    sends = []

    def edges(turn, low, high):
        copies = []
        for side, (row, to) in enumerate(((low, left), (high, right_of))):
            edge[turn, side] = row
            copy = pltpu.make_async_remote_copy(
                src_ref=edge.at[turn, side],
                dst_ref=edge_in.at[turn, side],
                send_sem=edge_send.at[turn, side],
                recv_sem=edge_recv.at[turn, side],
                device_id=(to, me),
                device_id_type=MESH,
            )
            copy.start()
            copies.append(copy)
            sends.append(copy)
        for copy in copies:
            copy.wait_recv()
        return edge_in[turn, 1], edge_in[turn, 0]

    def spread(buffer, inbox, send_sem, recv_sem, own, size, place):
        for d in range(1, size):
            copy = pltpu.make_async_remote_copy(
                src_ref=buffer,
                dst_ref=inbox.at[own],
                send_sem=send_sem.at[d],
                recv_sem=recv_sem.at[own],
                device_id=place(lax.rem(own + d, size)),
                device_id_type=MESH,
            )
            copy.start()
            sends.append(copy)
        inbox[own] = buffer[...]
        for d in range(1, size):
            other = lax.rem(own + d, size)
            pltpu.make_async_remote_copy(
                src_ref=buffer,
                dst_ref=inbox.at[other],
                send_sem=send_sem.at[d],
                recv_sem=recv_sem.at[other],
                device_id=place(other),
                device_id_type=MESH,
            ).wait_recv()

    low_lane = lax.broadcasted_iota(jnp.int32, (1, 2 * B), 1) < B

    def swap(row):
        return jnp.concatenate([row[:, B:], row[:, :B]], axis=1)

    def precondition(turn, t):
        z = []
        for l in range(2):
            lhs = jnp.broadcast_to(t[l], (8, 4 * B))
            z.append(mm(lhs, gz[l])[:1])
            sep[turn, pl.ds(l, 1), :] = mm(lhs, hh[l])[:1]
        spread(
            sep.at[turn], sep_in.at[turn], sep_send.at[turn], sep_recv.at[turn], me, ns, lambda s: (line, s)
        )
        out = []
        for l in range(2):
            g0, g1, g2, g3 = (sep_in[turn, s, pl.ds(l, 1), :] for s in range(4))
            f01 = jnp.where(low_lane, g0, g0 + swap(g1))
            f23 = g2 + jnp.where(low_lane, swap(g1), swap(g3))
            f = jnp.broadcast_to(jnp.concatenate([f01, f23], axis=1), (8, 4 * B))
            out.append(z[l] + mm(f, post[l])[:1])
        return out

    w = [weight[pl.ds(0, 1), :], weight[pl.ds(1, 1), :]]
    before_w, _ = edges(4, w[0], w[1])

    def across(turn, y):
        before, after = edges(turn, y[0], y[1])
        return [w[0] * y[1] + before_w * before, w[1] * after + w[0] * y[0]]

    ts = [[right[pl.ds(0, 1), :], right[pl.ds(1, 1), :]]]
    ys = []
    for turn in range(4):
        ys.append(precondition(turn, ts[turn]))
        ts.append(across(turn, ys[turn]))
    for i in range(8):
        y, t = ys[i // 2], ts[(i + 1) // 2]
        both = y[0] * t[0] + y[1] * t[1]
        sums[0, pl.ds(i, 1), :] = both[:, : 2 * B] + both[:, 2 * B :]
    for stage, (place, size, own) in enumerate(groups):
        spread(
            sums.at[stage], sums_in.at[stage], sum_send.at[stage], sum_recv.at[stage], own, size, place
        )
        total = sums_in[stage, 0]
        for i in range(1, size):
            total = total + sums_in[stage, i]
        sums[stage + 1] = total
    total = jnp.sum(total, axis=1, keepdims=True)
    g = [total[i : i + 1] for i in range(8)]
    m = [[g[i + j] for j in range(4)] + [-g[i + 4]] for i in range(4)]
    for k in range(3):
        inverse = 1.0 / m[k][k]
        for i in range(k + 1, 4):
            ratio = m[i][k] * inverse
            for j in range(k + 1, 5):
                m[i][j] = m[i][j] - ratio * m[k][j]
    d = [None] * 4 + [jnp.ones((1, 1), F32)]
    for k in (3, 2, 1, 0):
        value = m[k][4]
        for j in range(k + 1, 4):
            value = value - m[k][j] * d[j]
        d[k] = value / m[k][k]
    scale = 1.0 / (d[0] + d[1] + d[2] + d[3] + d[4])
    d = [value * scale for value in d]
    c = [None, None, None, d[4]]
    for k in (2, 1, 0):
        c[k] = c[k + 1] + d[k + 1]
    for l in range(2):
        x = c[0] * ys[0][l]
        r = d[0] * ts[0][l]
        for k in range(1, 4):
            x = x + c[k] * ys[k][l]
            r = r + d[k] * ts[k][l]
        out_x[pl.ds(l, 1), :] = x
        out_r[pl.ds(l, 1), :] = r + d[4] * ts[4][l]
    for copy in sends:
        copy.wait_send()


def local(diag_blocks, couplings, cross_weight, right_side):
    lines = right_side.shape[0]
    nl, ns = lax.axis_size("lines"), lax.axis_size("seg")
    ny = min(4, nl // 2)
    size = max(ns * ny, nl // ny)
    shape = jax.ShapeDtypeStruct
    gz, hh, xyz = pl.pallas_call(
        interior_kernel,
        out_shape=(
            shape((lines, 4 * B, 4 * B), F32),
            shape((lines, 4 * B, 2 * B), F32),
            shape((lines + 1, B, 2 * B), F32),
        ),
        in_specs=[VMEM] * 2,
        out_specs=[VMEM] * 3,
        scratch_shapes=[
            pltpu.VMEM((4 * B * lines, 2 * B), F32),
            pltpu.VMEM((4 * B * lines, 2 * B), F32),
            pltpu.VMEM((B * lines, 2 * B), F32),
        ],
        name="interior",
    )(diag_blocks, couplings)
    gathered = pl.pallas_call(
        gather_kernel,
        out_shape=shape((ns, lines + 1, B, 2 * B), F32),
        in_specs=[VMEM],
        out_specs=VMEM,
        scratch_shapes=[
            pltpu.VMEM((ns, lines + 1, B, 2 * B), F32),
            pltpu.SemaphoreType.DMA((ns - 1,)),
            pltpu.SemaphoreType.DMA((ns,)),
        ],
        compiler_params=pltpu.CompilerParams(collective_id=0, has_side_effects=True),
        name="gather",
    )(xyz)
    post = pl.pallas_call(
        reduced_kernel,
        out_shape=shape((lines, 4 * B, 4 * B), F32),
        in_specs=[VMEM] * 2,
        out_specs=VMEM,
        scratch_shapes=[
            pltpu.VMEM((B * lines, 2 * B), F32),
            pltpu.VMEM((5 * B, 4 * B), F32),
        ],
        name="reduced",
    )(gathered, hh)
    return pl.pallas_call(
        functools.partial(solve_kernel, (nl, ns, ny)),
        out_shape=(shape(right_side.shape, F32), shape(right_side.shape, F32)),
        in_specs=[VMEM] * 5,
        out_specs=[VMEM] * 2,
        scratch_shapes=[
            pltpu.VMEM((5, 2, 1, 4 * B), F32),
            pltpu.VMEM((5, 2, 1, 4 * B), F32),
            pltpu.VMEM((4, 8, 2 * B), F32),
            pltpu.VMEM((4, ns, 8, 2 * B), F32),
            pltpu.VMEM((3, 8, 2 * B), F32),
            pltpu.VMEM((2, size, 8, 2 * B), F32),
            pltpu.SemaphoreType.DMA((5, 2)),
            pltpu.SemaphoreType.DMA((5, 2)),
            pltpu.SemaphoreType.DMA((4, ns)),
            pltpu.SemaphoreType.DMA((4, ns)),
            pltpu.SemaphoreType.DMA((2, size)),
            pltpu.SemaphoreType.DMA((2, size)),
        ],
        compiler_params=pltpu.CompilerParams(collective_id=1, has_side_effects=True),
        name="solve",
    )(gz, hh, post, cross_weight, right_side)


def solution(mesh):
    return jax.shard_map(
        local,
        mesh=mesh,
        in_specs=(
            P("lines", "seg", None),
            P("lines", "seg", None),
            P("lines", "seg"),
            P("lines", "seg"),
        ),
        out_specs=(P("lines", "seg"), P("lines", "seg")),
        check_vma=False,
    )
```

```python
import functools

import jax
import jax.numpy as jnp
from jax import lax
from jax.experimental import pallas as pl
from jax.experimental.pallas import tpu as pltpu
from jax.sharding import PartitionSpec as P

B = 64
F32 = jnp.float32
BF16 = jnp.bfloat16
MESH = pl.DeviceIdType.MESH
EXACT = lax.Precision.HIGHEST


def mm(a, b):
    return jnp.dot(a, b, precision=EXACT, preferred_element_type=F32)


def mm_nt(a, b):
    return lax.dot_general(a, b, (((1,), (1,)), ((), ())), precision=EXACT, preferred_element_type=F32)


def iota(shape, dim):
    return lax.broadcasted_iota(jnp.int32, shape, dim)


def low_lanes(rows):
    return iota((rows, 2 * B), 1) < B


def swap(x):
    return jnp.concatenate([x[:, B:], x[:, :B]], axis=1)


def block_diag(pack):
    low = low_lanes(B)
    return jnp.concatenate([jnp.where(low, pack, 0.0), jnp.where(low, 0.0, pack)], axis=0)


def twice(x):
    return jnp.concatenate([x, x], axis=0)


def permuted(x):
    return jnp.concatenate([x[:, B : 2 * B], x[:, 3 * B :], x[:, 2 * B : 3 * B], x[:, :B]], axis=1)


def restored(x):
    return jnp.concatenate([x[:, 3 * B :], x[:, :B], x[:, 2 * B : 3 * B], x[:, B : 2 * B]], axis=1)


def row_of(x, j):
    return jnp.broadcast_to(x[j : j + 1], x.shape)


def invert(work, packs):
    shape = (8, 2 * B)
    sub, lane = iota(shape, 0), iota(shape, 1)
    half = jnp.where(lane < B, 0, B)

    def gather(x, at):
        return jnp.take_along_axis(x, at, axis=1, mode="promise_in_bounds")

    def panel(q, carry):
        base = 8 * q
        within = lane - half - base
        inside = jnp.logical_and(within >= 0, within < 8)
        unit = jnp.where(within == sub, 1.0, 0.0)
        at = [half + base + j for j in range(8)]
        rows = pl.ds(pl.multiple_of(base, 8), 8)
        for p in range(packs):
            r = work[p, rows, :]
            g = [gather(r, at[j]) for j in range(8)]
            r = jnp.where(inside, unit, r)
            for j in range(8):
                mine = sub == j
                inverse = 1.0 / row_of(g[j], j)
                scaled = row_of(r, j) * inverse
                r = jnp.where(mine, scaled, r - g[j] * scaled)
                for c in range(j + 1, 8):
                    scaled = row_of(g[c], j) * inverse
                    g[c] = jnp.where(mine, scaled, g[c] - g[j] * scaled)
            new = [row_of(r, j) for j in range(8)]
            for t in range(B // 8):
                tile = work[p, pl.ds(8 * t, 8), :]
                c = [gather(tile, at[j]) * new[j] for j in range(8)]
                total = ((c[0] + c[1]) + (c[2] + c[3])) + ((c[4] + c[5]) + (c[6] + c[7]))
                work[p, pl.ds(8 * t, 8), :] = jnp.where(inside, 0.0, tile) - total
            work[p, rows, :] = r
        return carry

    lax.fori_loop(0, B // 8, panel, 0)


def store_split(high, low, at, value):
    h = value.astype(BF16)
    high[at] = h
    low[at] = (value - h.astype(F32)).astype(BF16)


def apply(row, weights):
    wide = jnp.broadcast_to(row, (16, row.shape[1]))
    high = wide.astype(BF16).astype(F32)
    both = jnp.where(iota(wide.shape, 0) == 0, high, wide - high).astype(BF16)
    out = sum(jnp.dot(both, w, preferred_element_type=F32) for w in weights)
    return out[:1] + out[1:2]


def kernel(
    dims, diag, coup, weight, right, out_x, out_r,
    dch, pch, vec, in_d13, in_p10, in_d20, in_p23, in_vec, work, uq_s, et_s, xy_s,
    w1h, w1l, w2h, w2l, w3h, w3l, basis, edge_in, wbuf, mine, theirs, sums, sums_in,
    gat_send, gat_recv, edge_send, edge_recv, part_sem, sum_send, sum_recv,
):
    nl, ns, ny = dims
    m, s = lax.axis_index("lines"), lax.axis_index("seg")
    core, y_at, z_at = lax.rem(m, 2), lax.rem(m // 2, ny), m // (2 * ny)
    nz = nl // (2 * ny)

    def line_of(seg):
        return lax.rem(lax.rem((seg + 1) // 2, 2) + m, 2)

    b = line_of(s)
    mate = s + 1 - 2 * lax.rem(s, 2)
    partner = (m, mate)
    other = (lax.rem(m - 1 + 2 * b + nl, nl), s)
    others = [lax.rem(s + d, ns) for d in range(1, ns)]

    def near(index):
        return ((z_at * ny + index // 2) * 2 + core, (s // 2) * 2 + lax.rem(index, 2))

    def far(index):
        return (((index // 2) * ny + y_at) * 2 + lax.rem(index, 2), s)

    groups = ((near, 2 * ny, y_at * 2 + lax.rem(s, 2)), (far, 2 * nz, z_at * 2 + core))
    peers = [(m, x) for x in others] + [other]
    for place, size, own in groups:
        peers += [place(lax.rem(own + d, size)) for d in range(1, size)]
    barrier = pltpu.get_barrier_semaphore()
    for peer in peers:
        pl.semaphore_signal(barrier, inc=1, device_id=peer, device_id_type=MESH)

    not_first = iota((4, 2 * B), 0) > 0
    low4 = low_lanes(4)
    for l in range(2):
        for k in range(B // 2):
            cols = pl.ds(2 * B * k, 2 * B)
            edge = coup[l, :, cols]
            before = jnp.concatenate([edge[3:], edge[:3]], axis=0)
            full = diag[l, :, cols] + edge + jnp.where(not_first, before, 0.0)
            full_t, edge_t = swap(full), swap(edge)
            for dst, x, xt, order in ((dch, full, full_t, (2, 3, 0, 1)), (pch, edge, edge_t, (1, 0, 3, 2))):
                mate_x = jnp.concatenate([x[i : i + 1] for i in order], axis=0)
                mate_t = jnp.concatenate([xt[i : i + 1] for i in order], axis=0)
                dst[pl.ds(4 * B * l + 2 * k, 4, stride=B), :] = jnp.where(low4, x, mate_t)
                dst[pl.ds(4 * B * l + 2 * k + 1, 4, stride=B), :] = jnp.where(low4, xt, mate_x)
    vec[...] = jnp.concatenate([permuted(right[...]), permuted(weight[...])], axis=0)
    pl.semaphore_wait(barrier, len(peers))

    sends = []
    chunks = ((dch, 1, in_d13), (pch, 1, in_p10), (dch, 2, in_d20), (pch, 2, in_p23))

    def chunk_copy(i, to, slot, d):
        if i == len(chunks):
            src, dst = vec, in_vec
        else:
            array, e, dst = chunks[i]
            src = array.at[pl.ds(pl.multiple_of(4 * B * line_of(to) + B * e, B), B), :]
        return pltpu.make_async_remote_copy(
            src_ref=src,
            dst_ref=dst.at[slot],
            send_sem=gat_send.at[i, d],
            recv_sem=gat_recv.at[i, slot],
            device_id=(m, to),
            device_id_type=MESH,
        )

    for i in range(len(chunks) + 1):
        for d, to in enumerate(others):
            copy = chunk_copy(i, to, s, d)
            copy.start()
            sends.append(copy)

    def arrived(i):
        if i == len(chunks):
            in_vec[s] = vec[...]
        else:
            array, e, dst = chunks[i]
            dst[s] = array[pl.ds(pl.multiple_of(4 * B * b + B * e, B), B), :]
        for d, origin in enumerate(others):
            chunk_copy(i, origin, origin, d).wait_recv()

    low = low_lanes(B)
    runs = range(ns)
    arrived(0)
    invert(in_d13, ns)
    arrived(1)
    arrived(3)
    for r in runs:
        p10, p23 = in_p10[r], in_p23[r]
        if r == ns - 1:
            p23 = jnp.where(low, p23, 0.0)
        uq = mm(block_diag(in_d13[r]), jnp.concatenate([p10, p23], axis=0))
        uq_s[r] = uq
        a1 = mm(block_diag(p10), twice(uq[:B]))
        a3 = mm(block_diag(p23), twice(uq[B:]))
        if r == 0:
            arrived(2)
        d20 = in_d20[r]
        s2 = d20 - a1[:B] - a3[:B]
        if r % 2 == 0:
            work[r // 2] = s2
        else:
            work[r // 2] = jnp.where(low, work[r // 2], swap(s2))
        et_s[r] = jnp.where(low, swap(a3[:B]), a1[:B])
        xy_s[r] = jnp.where(low, swap(p23 - a3[B:]), d20 - a1[B:])
    arrived(4)
    invert(work, ns // 2)
    zs, zts, ss = [], [], []
    eye = jnp.where(iota((B, 2 * B), 0) + B == iota((B, 2 * B), 1), 1.0, 0.0)
    for r in runs:
        pack = work[r // 2]
        i2 = pack if r % 2 == 0 else swap(pack)
        et = et_s[r]
        ft = mm(i2[:, :B], et)
        cross = mm(et.T, ft)
        xy = xy_s[r] - jnp.where(low, cross[:B], cross[B:])
        zs.append(cross[B:, :B])
        zts.append(cross[:B, B:])
        ss.append(xy)
        uq = uq_s[r]
        ui = jnp.concatenate([uq[:, :B], eye[:, B:]], axis=0)
        t1 = mm(ui, jnp.concatenate([ft, i2[:, :B]], axis=1))
        t2 = mm_nt(t1[:, 2 * B :], ui)
        q0 = jnp.where(low, 0.0, uq[:B])
        q3 = jnp.where(low, swap(uq[B:]), 0.0)
        h = t1[:, : 2 * B] + jnp.concatenate([q0, q3, jnp.zeros((B, 2 * B), F32)], axis=0)
        h = jnp.concatenate([h, eye], axis=0)
        g = t2[: 2 * B, : 2 * B] + block_diag(in_d13[r])
        g = jnp.concatenate([g, t2[2 * B :, : 2 * B], jnp.zeros((B, 2 * B), F32)], axis=0)
        g2 = jnp.concatenate([t2[:, 2 * B :], jnp.zeros((B, B), F32)], axis=0)
        g2 = jnp.concatenate([g2, jnp.zeros((4 * B, B), F32)], axis=1)
        store_split(w1h, w1l, (r, slice(None), slice(0, 2 * B)), g)
        store_split(w1h, w1l, (r, slice(None), slice(2 * B, 4 * B)), g2)
        store_split(w1h, w1l, (r, slice(None), slice(4 * B, 6 * B)), h)
        ht = h.T
        w3h[r] = jnp.zeros((4 * B, 4 * B), BF16)
        w3l[r] = jnp.zeros((4 * B, 4 * B), BF16)
        store_split(w3h, w3l, (r, slice(B * r, B * r + B)), ht[B:])
        if r < ns - 1:
            store_split(w3h, w3l, (r, slice(B * r + B, B * r + 2 * B)), ht[:B])

    def separator(r):
        own = ss[r][:, B:]
        return own if r == 0 else own + ss[r - 1][:, :B]

    s0, s1, s2, s3 = (separator(r) for r in runs)
    work[0] = jnp.concatenate([s0, s3], axis=1)
    invert(work, 1)
    j0, j3 = work[0, :, :B], work[0, :, B:]
    v0, v3 = mm(j0, zs[0]), mm(j3, zts[2])
    s1 = s1 - mm(zts[0], v0)
    s2 = s2 - mm(zs[2], v3)
    work[0] = jnp.concatenate([s1, s2], axis=1)
    invert(work, 1)
    v12, v21 = mm(work[0, :, :B], zs[1]), mm(work[0, :, B:], zts[1])
    work[0] = jnp.concatenate([s1 - mm(zs[1], v21), s2 - mm(zts[1], v12)], axis=1)
    invert(work, 1)
    e11, e22 = work[0, :, :B], work[0, :, B:]
    e12, e21 = mm(v12, e22), mm(v21, e11)
    inner = jnp.concatenate(
        [jnp.concatenate([e11, e12], axis=1), jnp.concatenate([e21, e22], axis=1)], axis=0
    )
    zero = jnp.zeros((B, B), F32)
    v = jnp.concatenate([jnp.concatenate([v0, zero], axis=1), jnp.concatenate([zero, v3], axis=1)], axis=0)
    side = mm(v, inner)
    corner = mm_nt(side, v)
    back = mm_nt(inner, v)
    rows = (
        jnp.concatenate([j0 + corner[:B, :B], side[:B], corner[:B, B:]], axis=1),
        jnp.concatenate([back[:B, :B], inner[:B], back[:B, B:]], axis=1),
        jnp.concatenate([back[B:, :B], inner[B:], back[B:, B:]], axis=1),
        jnp.concatenate([corner[B:, :B], side[B:], j3 + corner[B:, B:]], axis=1),
    )
    for r in runs:
        after = rows[r + 1] if r + 1 < ns else jnp.zeros((B, 4 * B), F32)
        store_split(w2h, w2l, (slice(2 * B * r, 2 * B * r + B),), after)
        store_split(w2h, w2l, (slice(2 * B * r + B, 2 * B * r + 2 * B),), rows[r])

    def solve(t):
        first = [apply(t[r : r + 1], (w1h[r], w1l[r])) for r in runs]
        f = jnp.concatenate([x[:, 4 * B :] for x in first], axis=1)
        u = apply(f, (w2h[...], w2l[...]))
        out = [first[r][:, : 4 * B] + apply(u, (w3h[r], w3l[r])) for r in runs]
        return jnp.concatenate(out, axis=0)

    def exchange(turn, source, targets):
        copies = []
        for side, to in targets:
            copy = pltpu.make_async_remote_copy(
                src_ref=source,
                dst_ref=edge_in.at[turn, side],
                send_sem=edge_send.at[turn, side],
                recv_sem=edge_recv.at[turn, side],
                device_id=to,
                device_id_type=MESH,
            )
            copy.start()
            copies.append(copy)
            sends.append(copy)
        for copy in copies:
            copy.wait_recv()

    w_mate = jnp.concatenate([in_vec[r, pl.ds(2, 1), :] for r in runs], axis=0)
    w_own = jnp.concatenate([in_vec[r, pl.ds(3, 1), :] for r in runs], axis=0)
    wbuf[...] = w_own
    exchange(4, wbuf, ((1, other),))
    w_other = jnp.where(b == 0, edge_in[4, 1], w_own)
    t = jnp.concatenate([in_vec[r, pl.ds(b, 1), :] for r in runs], axis=0)
    ts, ys = [t], []
    basis[4] = t
    for turn in range(4):
        ys.append(solve(ts[turn]))
        basis[turn] = ys[turn]
        exchange(turn, basis.at[turn], ((0, partner), (1, other)))
        ts.append(w_mate * edge_in[turn, 0] + w_other * edge_in[turn, 1])
        basis[5 + turn] = ts[turn + 1]
    for j in range(9):
        mine[pl.ds(j, 1), :] = basis[j, pl.ds(mate, 1), :]
    swap_copy = pltpu.make_async_remote_copy(
        src_ref=mine,
        dst_ref=theirs,
        send_sem=part_sem.at[0],
        recv_sem=part_sem.at[1],
        device_id=partner,
        device_id_type=MESH,
    )
    for i in range(8):
        both = jnp.sum(ys[i // 2] * ts[(i + 1) // 2], axis=0, keepdims=True)
        sums[0, pl.ds(i, 1), :] = both[:, : 2 * B] + both[:, 2 * B :]
    for stage, (place, size, own) in enumerate(groups):
        for d in range(1, size):
            copy = pltpu.make_async_remote_copy(
                src_ref=sums.at[stage],
                dst_ref=sums_in.at[stage, own],
                send_sem=sum_send.at[stage, d],
                recv_sem=sum_recv.at[stage, own],
                device_id=place(lax.rem(own + d, size)),
                device_id_type=MESH,
            )
            copy.start()
            sends.append(copy)
        if stage == 0:
            swap_copy.start()
        sums_in[stage, own] = sums[stage]
        for d in range(1, size):
            origin = lax.rem(own + d, size)
            pltpu.make_async_remote_copy(
                src_ref=sums.at[stage],
                dst_ref=sums_in.at[stage, origin],
                send_sem=sum_send.at[stage, d],
                recv_sem=sum_recv.at[stage, origin],
                device_id=place(origin),
                device_id_type=MESH,
            ).wait_recv()
        total = sums_in[stage, 0]
        for i in range(1, size):
            total = total + sums_in[stage, i]
        sums[stage + 1] = total
    total = jnp.sum(total, axis=1, keepdims=True)
    moments = [total[i : i + 1] for i in range(8)]
    a = [[moments[i + j] for j in range(4)] + [-moments[i + 4]] for i in range(4)]
    for k in range(3):
        inverse = 1.0 / a[k][k]
        for i in range(k + 1, 4):
            ratio = a[i][k] * inverse
            for j in range(k + 1, 5):
                a[i][j] = a[i][j] - ratio * a[k][j]
    d = [None] * 4 + [jnp.ones((1, 1), F32)]
    for k in (3, 2, 1, 0):
        value = a[k][4]
        for j in range(k + 1, 4):
            value = value - a[k][j] * d[j]
        d[k] = value / a[k][k]
    scale = 1.0 / (d[0] + d[1] + d[2] + d[3] + d[4])
    d = [value * scale for value in d]
    c = [None, None, None, d[4]]
    for k in (2, 1, 0):
        c[k] = c[k + 1] + d[k + 1]

    def combine(part):
        x, r = c[0] * part(0), d[0] * part(4)
        for k in range(1, 4):
            x = x + c[k] * part(k)
        for k in range(1, 5):
            r = r + d[k] * part(4 + k)
        return restored(x), restored(r)

    x_mine, r_mine = combine(lambda j: basis[j, pl.ds(s, 1), :])
    swap_copy.wait()
    x_theirs, r_theirs = combine(lambda j: theirs[pl.ds(j, 1), :])
    first = b == 0
    out_x[pl.ds(0, 1), :] = jnp.where(first, x_mine, x_theirs)
    out_x[pl.ds(1, 1), :] = jnp.where(first, x_theirs, x_mine)
    out_r[pl.ds(0, 1), :] = jnp.where(first, r_mine, r_theirs)
    out_r[pl.ds(1, 1), :] = jnp.where(first, r_theirs, r_mine)
    for copy in sends:
        copy.wait_send()


def local(diag_blocks, couplings, cross_weight, right_side):
    nl, ns = lax.axis_size("lines"), lax.axis_size("seg")
    ny = min(4, nl // 2)
    size = max(2 * ny, nl // ny)
    shape = jax.ShapeDtypeStruct
    block = pl.BlockSpec(memory_space=pltpu.VMEM)
    vmem, dma = pltpu.VMEM, pltpu.SemaphoreType.DMA
    return pl.pallas_call(
        functools.partial(kernel, (nl, ns, ny)),
        out_shape=(shape(right_side.shape, F32), shape(right_side.shape, F32)),
        in_specs=[block] * 4,
        out_specs=[block] * 2,
        scratch_shapes=[
            vmem((8 * B, 2 * B), F32),
            vmem((8 * B, 2 * B), F32),
            vmem((4, 4 * B), F32),
            vmem((ns, B, 2 * B), F32),
            vmem((ns, B, 2 * B), F32),
            vmem((ns, B, 2 * B), F32),
            vmem((ns, B, 2 * B), F32),
            vmem((ns, 4, 4 * B), F32),
            vmem((ns // 2, B, 2 * B), F32),
            vmem((ns, 2 * B, 2 * B), F32),
            vmem((ns, B, 2 * B), F32),
            vmem((ns, B, 2 * B), F32),
            vmem((ns, 4 * B, 6 * B), BF16),
            vmem((ns, 4 * B, 6 * B), BF16),
            vmem((8 * B, 4 * B), BF16),
            vmem((8 * B, 4 * B), BF16),
            vmem((ns, 4 * B, 4 * B), BF16),
            vmem((ns, 4 * B, 4 * B), BF16),
            vmem((9, 4, 4 * B), F32),
            vmem((5, 2, 4, 4 * B), F32),
            vmem((4, 4 * B), F32),
            vmem((16, 4 * B), F32),
            vmem((16, 4 * B), F32),
            vmem((3, 8, 2 * B), F32),
            vmem((2, size, 8, 2 * B), F32),
            dma((5, ns)),
            dma((5, ns)),
            dma((5, 2)),
            dma((5, 2)),
            dma((2,)),
            dma((2, size)),
            dma((2, size)),
        ],
        compiler_params=pltpu.CompilerParams(
            collective_id=0, has_side_effects=True, vmem_limit_bytes=40 * 2**20
        ),
        name="line_cg",
    )(diag_blocks, couplings, cross_weight, right_side)


def solution(mesh):
    return jax.shard_map(
        local,
        mesh=mesh,
        in_specs=(
            P("lines", "seg", None),
            P("lines", "seg", None),
            P("lines", "seg"),
            P("lines", "seg"),
        ),
        out_specs=(P("lines", "seg"), P("lines", "seg")),
        check_vma=False,
    )
```

```python
import functools

import jax
import jax.numpy as jnp
from jax import lax
from jax.experimental import pallas as pl
from jax.experimental.pallas import tpu as pltpu
from jax.sharding import PartitionSpec as P

B = 64
F32 = jnp.float32
BF16 = jnp.bfloat16
MESH = pl.DeviceIdType.MESH
EXACT = lax.Precision.HIGHEST


def mm(a, b):
    return jnp.dot(a, b, precision=EXACT, preferred_element_type=F32)


def mm_nt(a, b):
    return lax.dot_general(a, b, (((1,), (1,)), ((), ())), precision=EXACT, preferred_element_type=F32)


def iota(shape, dim):
    return lax.broadcasted_iota(jnp.int32, shape, dim)


def low_lanes(rows):
    return iota((rows, 2 * B), 1) < B


def swap(x):
    return jnp.concatenate([x[:, B:], x[:, :B]], axis=1)


def block_diag(pack):
    low = low_lanes(B)
    return jnp.concatenate([jnp.where(low, pack, 0.0), jnp.where(low, 0.0, pack)], axis=0)


def twice(x):
    return jnp.concatenate([x, x], axis=0)


def permuted(x):
    return jnp.concatenate([x[:, B : 2 * B], x[:, 3 * B :], x[:, 2 * B : 3 * B], x[:, :B]], axis=1)


def restored(x):
    return jnp.concatenate([x[:, 3 * B :], x[:, :B], x[:, 2 * B : 3 * B], x[:, B : 2 * B]], axis=1)


def row_of(x, j):
    return jnp.broadcast_to(x[j : j + 1], x.shape)


def invert(work, packs):
    shape = (8, 2 * B)
    sub, lane = iota(shape, 0), iota(shape, 1)
    low = lane < B
    half = jnp.where(low, 0, B)
    lane_all = iota((B, 2 * B), 1)
    half_all = jnp.where(lane_all < B, 0, B)
    none = jnp.zeros(shape, F32)
    every = range(packs)

    def gather(x, at):
        return [jnp.take_along_axis(x, i, axis=1, mode="promise_in_bounds") for i in at]

    whole = [work[p] for p in every]
    rows = [x[:8] for x in whole]
    for q in range(B // 8):
        base = 8 * q
        within = lane - half - base
        inside = jnp.logical_and(within >= 0, within < 8)
        within_all = lane_all - half_all - base
        inside_all = jnp.logical_and(within_all >= 0, within_all < 8)
        at = [half + base + j for j in range(8)]
        cols = [gather(r, at) for r in rows]
        more = q + 1 < B // 8
        if more:
            after = [x[base + 8 : base + 16] for x in whole]
            after_cols = [gather(x, at) for x in after]
        rows = [jnp.where(inside, jnp.where(within == sub, 1.0, 0.0), r) for r in rows]
        scale = [none for _ in every]
        for j in range(8):
            mine = sub == j
            for p in every:
                g = cols[p]
                inverse = 1.0 / row_of(g[j], j)
                ratio = jnp.where(mine, 0.0, g[j]) * inverse
                scale[p] = jnp.where(mine, inverse, scale[p])
                for c in range(j + 1, 8):
                    g[c] = g[c] - ratio * row_of(g[c], j)
                rows[p] = rows[p] - ratio * row_of(rows[p], j)
        for p in every:
            new = rows[p] * scale[p]
            left, right = jnp.where(low, new, 0.0), jnp.where(low, 0.0, new)
            weights = jnp.concatenate([none] * q + [left] + [none] * 7 + [right] + [none] * (7 - q), axis=0)
            rest = jnp.where(inside_all, 0.0, whole[p]) - mm(jnp.where(inside_all, whole[p], 0.0), weights)
            parts = ([rest[:base]] if q else []) + [new] + ([rest[base + 8 :]] if more else [])
            whole[p] = jnp.concatenate(parts, axis=0)
            if more:
                c = [after_cols[p][j] * row_of(new, j) for j in range(8)]
                total = ((c[0] + c[1]) + (c[2] + c[3])) + ((c[4] + c[5]) + (c[6] + c[7]))
                rows[p] = jnp.where(inside, 0.0, after[p]) - total
    for p in every:
        work[p] = whole[p]


def store_split(high, low, at, value):
    h = value.astype(BF16)
    high[at] = h
    low[at] = (value - h.astype(F32)).astype(BF16)


def apply(row, weights):
    wide = jnp.broadcast_to(row, (16, row.shape[1]))
    high = wide.astype(BF16).astype(F32)
    both = jnp.where(iota(wide.shape, 0) == 0, high, wide - high).astype(BF16)
    out = sum(jnp.dot(both, w, preferred_element_type=F32) for w in weights)
    return out[:1] + out[1:2]


def kernel(
    dims, diag_in, coup_in, weight_in, right_in, out_x, out_r, diag, coup, weight, right, in_sem,
    dch, pch, vec, in_d13, in_p10, in_d20, in_p23, in_vec, work, uq_s, et_s, xy_s,
    w1h, w1l, w2h, w2l, w3h, w3l, basis, edge_in, wbuf, mine, theirs, sums, sums_in,
    gat_send, gat_recv, edge_send, edge_recv, part_sem, sum_send, sum_recv,
):
    nl, ns, ny = dims
    m, s = lax.axis_index("lines"), lax.axis_index("seg")
    core, y_at, z_at = lax.rem(m, 2), lax.rem(m // 2, ny), m // (2 * ny)
    nz = nl // (2 * ny)

    def line_of(seg):
        return lax.rem(lax.rem((seg + 1) // 2, 2) + m, 2)

    b = line_of(s)
    mate = s + 1 - 2 * lax.rem(s, 2)
    partner = (m, mate)
    other = (lax.rem(m - 1 + 2 * b + nl, nl), s)
    others = [lax.rem(s + d, ns) for d in range(1, ns)]

    def near(index):
        return (z_at * ny * 2 + index // 2, (s // 2) * 2 + lax.rem(index, 2))

    def far(index):
        return ((index * ny + y_at) * 2 + core, s)

    groups = ((near, 4 * ny, (y_at * 2 + core) * 2 + lax.rem(s, 2)), (far, nz, z_at))
    peers = [(m, x) for x in others] + [other]
    for place, size, own in groups:
        peers += [place(lax.rem(own + d, size)) for d in range(1, size)]
    pairs = ((diag_in, diag), (coup_in, coup), (weight_in, weight), (right_in, right))
    loads = [pltpu.make_async_copy(src, dst, in_sem.at[i]) for i, (src, dst) in enumerate(pairs)]
    for load in loads:
        load.start()
    barrier = pltpu.get_barrier_semaphore()
    for peer in peers:
        pl.semaphore_signal(barrier, inc=1, device_id=peer, device_id_type=MESH)

    not_first = iota((4, 2 * B), 0) > 0
    low4 = low_lanes(4)

    def lay_out(dst, tile_of, order):
        for l in range(2):
            for k in range(B // 2):
                x = tile_of(l, pl.ds(2 * B * k, 2 * B))
                xt = swap(x)
                mate_x = jnp.concatenate([x[i : i + 1] for i in order], axis=0)
                mate_t = jnp.concatenate([xt[i : i + 1] for i in order], axis=0)
                dst[pl.ds(4 * B * l + 2 * k, 4, stride=B), :] = jnp.where(low4, x, mate_t)
                dst[pl.ds(4 * B * l + 2 * k + 1, 4, stride=B), :] = jnp.where(low4, xt, mate_x)

    def diagonal(l, cols):
        edge = coup[l, :, cols]
        before = jnp.concatenate([edge[3:], edge[:3]], axis=0)
        return diag[l, :, cols] + edge + jnp.where(not_first, before, 0.0)

    loads[0].wait()
    loads[1].wait()
    lay_out(dch, diagonal, (2, 3, 0, 1))
    pl.semaphore_wait(barrier, len(peers))

    sends = []
    chunks = ((dch, 1, in_d13), (pch, 1, in_p10), (dch, 2, in_d20), (pch, 2, in_p23))

    def chunk_copy(i, to, slot, d):
        if i == len(chunks):
            src, dst = vec, in_vec
        else:
            array, e, dst = chunks[i]
            src = array.at[pl.ds(pl.multiple_of(4 * B * line_of(to) + B * e, B), B), :]
        return pltpu.make_async_remote_copy(
            src_ref=src,
            dst_ref=dst.at[slot],
            send_sem=gat_send.at[i, d],
            recv_sem=gat_recv.at[i, slot],
            device_id=(m, to),
            device_id_type=MESH,
        )

    def send_chunk(i):
        for d, to in enumerate(others):
            copy = chunk_copy(i, to, s, d)
            copy.start()
            sends.append(copy)

    send_chunk(0)
    lay_out(pch, lambda l, cols: coup[l, :, cols], (1, 0, 3, 2))
    send_chunk(1)
    send_chunk(3)
    loads[2].wait()
    loads[3].wait()
    vec[...] = jnp.concatenate([permuted(right[...]), permuted(weight[...])], axis=0)
    send_chunk(4)
    send_chunk(2)

    def arrived(i):
        if i == len(chunks):
            in_vec[s] = vec[...]
        else:
            array, e, dst = chunks[i]
            dst[s] = array[pl.ds(pl.multiple_of(4 * B * b + B * e, B), B), :]
        for d, origin in enumerate(others):
            chunk_copy(i, origin, origin, d).wait_recv()

    def exchange(turn, source, targets):
        copies = []
        for side, to in targets:
            copy = pltpu.make_async_remote_copy(
                src_ref=source,
                dst_ref=edge_in.at[turn, side],
                send_sem=edge_send.at[turn, side],
                recv_sem=edge_recv.at[turn, side],
                device_id=to,
                device_id_type=MESH,
            )
            copy.start()
            copies.append(copy)
            sends.append(copy)

        def finish():
            for copy in copies:
                copy.wait_recv()

        return finish

    low = low_lanes(B)
    runs = range(ns)
    arrived(0)
    invert(in_d13, ns)
    arrived(1)
    arrived(3)
    for r in runs:
        p10, p23 = in_p10[r], in_p23[r]
        if r == ns - 1:
            p23 = jnp.where(low, p23, 0.0)
        uq = mm(block_diag(in_d13[r]), jnp.concatenate([p10, p23], axis=0))
        uq_s[r] = uq
        a1 = mm(block_diag(p10), twice(uq[:B]))
        a3 = mm(block_diag(p23), twice(uq[B:]))
        if r == 0:
            arrived(2)
        d20 = in_d20[r]
        s2 = d20 - a1[:B] - a3[:B]
        if r % 2 == 0:
            work[r // 2] = s2
        else:
            work[r // 2] = jnp.where(low, work[r // 2], swap(s2))
        et_s[r] = jnp.where(low, swap(a3[:B]), a1[:B])
        xy_s[r] = jnp.where(low, swap(p23 - a3[B:]), d20 - a1[B:])
    arrived(4)
    w_mate = jnp.concatenate([in_vec[r, pl.ds(2, 1), :] for r in runs], axis=0)
    w_own = jnp.concatenate([in_vec[r, pl.ds(3, 1), :] for r in runs], axis=0)
    wbuf[...] = w_own
    wait_weights = exchange(4, wbuf, ((1, other),))
    invert(work, ns // 2)
    zs, zts, ss = [], [], []
    eye = jnp.where(iota((B, 2 * B), 0) + B == iota((B, 2 * B), 1), 1.0, 0.0)
    for r in runs:
        pack = work[r // 2]
        i2 = pack if r % 2 == 0 else swap(pack)
        et = et_s[r]
        ft = mm(i2[:, :B], et)
        cross = mm(et.T, ft)
        xy = xy_s[r] - jnp.where(low, cross[:B], cross[B:])
        zs.append(cross[B:, :B])
        zts.append(cross[:B, B:])
        ss.append(xy)
        uq = uq_s[r]
        ui = jnp.concatenate([uq[:, :B], eye[:, B:]], axis=0)
        t1 = mm(ui, jnp.concatenate([ft, i2[:, :B]], axis=1))
        t2 = mm_nt(t1[:, 2 * B :], ui)
        q0 = jnp.where(low, 0.0, uq[:B])
        q3 = jnp.where(low, swap(uq[B:]), 0.0)
        h = t1[:, : 2 * B] + jnp.concatenate([q0, q3, jnp.zeros((B, 2 * B), F32)], axis=0)
        h = jnp.concatenate([h, eye], axis=0)
        g = t2[: 2 * B, : 2 * B] + block_diag(in_d13[r])
        g = jnp.concatenate([g, t2[2 * B :, : 2 * B], jnp.zeros((B, 2 * B), F32)], axis=0)
        g2 = jnp.concatenate([t2[:, 2 * B :], jnp.zeros((B, B), F32)], axis=0)
        g2 = jnp.concatenate([g2, jnp.zeros((4 * B, B), F32)], axis=1)
        store_split(w1h, w1l, (r, slice(None), slice(0, 2 * B)), g)
        store_split(w1h, w1l, (r, slice(None), slice(2 * B, 4 * B)), g2)
        store_split(w1h, w1l, (r, slice(None), slice(4 * B, 6 * B)), h)
        ht = h.T
        w3h[r] = jnp.zeros((4 * B, 4 * B), BF16)
        w3l[r] = jnp.zeros((4 * B, 4 * B), BF16)
        store_split(w3h, w3l, (r, slice(B * r, B * r + B)), ht[B:])
        if r < ns - 1:
            store_split(w3h, w3l, (r, slice(B * r + B, B * r + 2 * B)), ht[:B])

    def separator(r):
        own = ss[r][:, B:]
        return own if r == 0 else own + ss[r - 1][:, :B]

    s0, s1, s2, s3 = (separator(r) for r in runs)
    work[0] = jnp.concatenate([s0, s3], axis=1)
    invert(work, 1)
    j0, j3 = work[0, :, :B], work[0, :, B:]
    v0, v3 = mm(j0, zs[0]), mm(j3, zts[2])
    s1 = s1 - mm(zts[0], v0)
    s2 = s2 - mm(zs[2], v3)
    work[0] = jnp.concatenate([s1, s2], axis=1)
    invert(work, 1)
    v12, v21 = mm(work[0, :, :B], zs[1]), mm(work[0, :, B:], zts[1])
    work[0] = jnp.concatenate([s1 - mm(zs[1], v21), s2 - mm(zts[1], v12)], axis=1)
    invert(work, 1)
    e11, e22 = work[0, :, :B], work[0, :, B:]
    e12, e21 = mm(v12, e22), mm(v21, e11)
    inner = jnp.concatenate(
        [jnp.concatenate([e11, e12], axis=1), jnp.concatenate([e21, e22], axis=1)], axis=0
    )
    zero = jnp.zeros((B, B), F32)
    v = jnp.concatenate([jnp.concatenate([v0, zero], axis=1), jnp.concatenate([zero, v3], axis=1)], axis=0)
    side = mm(v, inner)
    corner = mm_nt(side, v)
    back = mm_nt(inner, v)
    rows = (
        jnp.concatenate([j0 + corner[:B, :B], side[:B], corner[:B, B:]], axis=1),
        jnp.concatenate([back[:B, :B], inner[:B], back[:B, B:]], axis=1),
        jnp.concatenate([back[B:, :B], inner[B:], back[B:, B:]], axis=1),
        jnp.concatenate([corner[B:, :B], side[B:], j3 + corner[B:, B:]], axis=1),
    )
    for r in runs:
        after = rows[r + 1] if r + 1 < ns else jnp.zeros((B, 4 * B), F32)
        store_split(w2h, w2l, (slice(2 * B * r, 2 * B * r + B),), after)
        store_split(w2h, w2l, (slice(2 * B * r + B, 2 * B * r + 2 * B),), rows[r])

    def solve(t):
        first = [apply(t[r : r + 1], (w1h[r], w1l[r])) for r in runs]
        f = jnp.concatenate([x[:, 4 * B :] for x in first], axis=1)
        u = apply(f, (w2h[...], w2l[...]))
        out = [first[r][:, : 4 * B] + apply(u, (w3h[r], w3l[r])) for r in runs]
        return jnp.concatenate(out, axis=0)

    t = jnp.concatenate([in_vec[r, pl.ds(b, 1), :] for r in runs], axis=0)
    ts, ys = [t], []
    basis[4] = t
    for turn in range(4):
        ys.append(solve(ts[turn]))
        basis[turn] = ys[turn]
        arrive = exchange(turn, basis.at[turn], ((0, partner), (1, other)))
        if turn == 0:
            wait_weights()
            w_other = jnp.where(b == 0, edge_in[4, 1], w_own)
        arrive()
        ts.append(w_mate * edge_in[turn, 0] + w_other * edge_in[turn, 1])
        basis[5 + turn] = ts[turn + 1]
    for j in range(9):
        mine[pl.ds(j, 1), :] = basis[j, pl.ds(mate, 1), :]
    swap_copy = pltpu.make_async_remote_copy(
        src_ref=mine,
        dst_ref=theirs,
        send_sem=part_sem.at[0],
        recv_sem=part_sem.at[1],
        device_id=partner,
        device_id_type=MESH,
    )
    for i in range(8):
        both = jnp.sum(ys[i // 2] * ts[(i + 1) // 2], axis=0, keepdims=True)
        sums[0, pl.ds(i, 1), :] = both[:, : 2 * B] + both[:, 2 * B :]
    for stage, (place, size, own) in enumerate(groups):
        for d in range(1, size):
            copy = pltpu.make_async_remote_copy(
                src_ref=sums.at[stage],
                dst_ref=sums_in.at[stage, own],
                send_sem=sum_send.at[stage, d],
                recv_sem=sum_recv.at[stage, own],
                device_id=place(lax.rem(own + d, size)),
                device_id_type=MESH,
            )
            copy.start()
            sends.append(copy)
        if stage == 0:
            swap_copy.start()
        sums_in[stage, own] = sums[stage]
        for d in range(1, size):
            origin = lax.rem(own + d, size)
            pltpu.make_async_remote_copy(
                src_ref=sums.at[stage],
                dst_ref=sums_in.at[stage, origin],
                send_sem=sum_send.at[stage, d],
                recv_sem=sum_recv.at[stage, origin],
                device_id=place(origin),
                device_id_type=MESH,
            ).wait_recv()
        total = sums_in[stage, 0]
        for i in range(1, size):
            total = total + sums_in[stage, i]
        sums[stage + 1] = total
    total = jnp.sum(total, axis=1, keepdims=True)
    moments = [total[i : i + 1] for i in range(8)]
    a = [[moments[i + j] for j in range(4)] + [-moments[i + 4]] for i in range(4)]
    for k in range(3):
        inverse = 1.0 / a[k][k]
        for i in range(k + 1, 4):
            ratio = a[i][k] * inverse
            for j in range(k + 1, 5):
                a[i][j] = a[i][j] - ratio * a[k][j]
    d = [None] * 4 + [jnp.ones((1, 1), F32)]
    for k in (3, 2, 1, 0):
        value = a[k][4]
        for j in range(k + 1, 4):
            value = value - a[k][j] * d[j]
        d[k] = value / a[k][k]
    scale = 1.0 / (d[0] + d[1] + d[2] + d[3] + d[4])
    d = [value * scale for value in d]
    c = [None, None, None, d[4]]
    for k in (2, 1, 0):
        c[k] = c[k + 1] + d[k + 1]

    def combine(part):
        x, r = c[0] * part(0), d[0] * part(4)
        for k in range(1, 4):
            x = x + c[k] * part(k)
        for k in range(1, 5):
            r = r + d[k] * part(4 + k)
        return restored(x), restored(r)

    x_mine, r_mine = combine(lambda j: basis[j, pl.ds(s, 1), :])
    swap_copy.wait()
    x_theirs, r_theirs = combine(lambda j: theirs[pl.ds(j, 1), :])
    first = b == 0
    out_x[pl.ds(0, 1), :] = jnp.where(first, x_mine, x_theirs)
    out_x[pl.ds(1, 1), :] = jnp.where(first, x_theirs, x_mine)
    out_r[pl.ds(0, 1), :] = jnp.where(first, r_mine, r_theirs)
    out_r[pl.ds(1, 1), :] = jnp.where(first, r_theirs, r_mine)
    for copy in sends:
        copy.wait_send()


def local(diag_blocks, couplings, cross_weight, right_side):
    nl, ns = lax.axis_size("lines"), lax.axis_size("seg")
    ny = min(4, nl // 2)
    size = max(4 * ny, nl // (2 * ny))
    shape = jax.ShapeDtypeStruct
    block = pl.BlockSpec(memory_space=pltpu.VMEM)
    vmem, dma = pltpu.VMEM, pltpu.SemaphoreType.DMA
    return pl.pallas_call(
        functools.partial(kernel, (nl, ns, ny)),
        out_shape=(shape(right_side.shape, F32), shape(right_side.shape, F32)),
        in_specs=[pl.BlockSpec(memory_space=pltpu.HBM)] * 4,
        out_specs=[block] * 2,
        scratch_shapes=[
            vmem(diag_blocks.shape, F32),
            vmem(couplings.shape, F32),
            vmem(cross_weight.shape, F32),
            vmem(right_side.shape, F32),
            dma((4,)),
            vmem((8 * B, 2 * B), F32),
            vmem((8 * B, 2 * B), F32),
            vmem((4, 4 * B), F32),
            vmem((ns, B, 2 * B), F32),
            vmem((ns, B, 2 * B), F32),
            vmem((ns, B, 2 * B), F32),
            vmem((ns, B, 2 * B), F32),
            vmem((ns, 4, 4 * B), F32),
            vmem((ns // 2, B, 2 * B), F32),
            vmem((ns, 2 * B, 2 * B), F32),
            vmem((ns, B, 2 * B), F32),
            vmem((ns, B, 2 * B), F32),
            vmem((ns, 4 * B, 6 * B), BF16),
            vmem((ns, 4 * B, 6 * B), BF16),
            vmem((8 * B, 4 * B), BF16),
            vmem((8 * B, 4 * B), BF16),
            vmem((ns, 4 * B, 4 * B), BF16),
            vmem((ns, 4 * B, 4 * B), BF16),
            vmem((9, 4, 4 * B), F32),
            vmem((5, 2, 4, 4 * B), F32),
            vmem((4, 4 * B), F32),
            vmem((16, 4 * B), F32),
            vmem((16, 4 * B), F32),
            vmem((3, 8, 2 * B), F32),
            vmem((2, size, 8, 2 * B), F32),
            dma((5, ns)),
            dma((5, ns)),
            dma((5, 2)),
            dma((5, 2)),
            dma((2,)),
            dma((2, size)),
            dma((2, size)),
        ],
        compiler_params=pltpu.CompilerParams(
            collective_id=0, has_side_effects=True
        ),
        name="line_cg",
    )(diag_blocks, couplings, cross_weight, right_side)


def solution(mesh):
    return jax.shard_map(
        local,
        mesh=mesh,
        in_specs=(
            P("lines", "seg", None),
            P("lines", "seg", None),
            P("lines", "seg"),
            P("lines", "seg"),
        ),
        out_specs=(P("lines", "seg"), P("lines", "seg")),
        check_vma=False,
    )
```

```python
import functools

import jax
import jax.numpy as jnp
from jax import lax
from jax.experimental import pallas as pl
from jax.experimental.pallas import tpu as pltpu
from jax.sharding import PartitionSpec as P

B = 64
F32 = jnp.float32
BF16 = jnp.bfloat16
MESH = pl.DeviceIdType.MESH
EXACT = lax.Precision.HIGHEST


def mm(a, b):
    return jnp.dot(a, b, precision=EXACT, preferred_element_type=F32)


def mm_nt(a, b):
    return lax.dot_general(a, b, (((1,), (1,)), ((), ())), precision=EXACT, preferred_element_type=F32)


def iota(shape, dim):
    return lax.broadcasted_iota(jnp.int32, shape, dim)


def low_lanes(rows):
    return iota((rows, 2 * B), 1) < B


def swap(x):
    return jnp.concatenate([x[:, B:], x[:, :B]], axis=1)


def block_diag(pack):
    low = low_lanes(B)
    return jnp.concatenate([jnp.where(low, pack, 0.0), jnp.where(low, 0.0, pack)], axis=0)


def twice(x):
    return jnp.concatenate([x, x], axis=0)


def permuted(x):
    return jnp.concatenate([x[:, B : 2 * B], x[:, 3 * B :], x[:, 2 * B : 3 * B], x[:, :B]], axis=1)


def restored(x):
    return jnp.concatenate([x[:, 3 * B :], x[:, :B], x[:, 2 * B : 3 * B], x[:, B : 2 * B]], axis=1)


def row_of(x, j):
    return jnp.broadcast_to(x[j : j + 1], x.shape)


def invert(work, packs):
    shape = (8, 2 * B)
    sub, lane = iota(shape, 0), iota(shape, 1)
    low = lane < B
    half = jnp.where(low, 0, B)
    lane_all = iota((B, 2 * B), 1)
    half_all = jnp.where(lane_all < B, 0, B)
    none = jnp.zeros(shape, F32)
    every = range(packs)

    def gather(x, at):
        return [jnp.take_along_axis(x, i, axis=1, mode="promise_in_bounds") for i in at]

    def less(x, x_cols, new, inside):
        c = [x_cols[j] * row_of(new, j) for j in range(8)]
        total = ((c[0] + c[1]) + (c[2] + c[3])) + ((c[4] + c[5]) + (c[6] + c[7]))
        return jnp.where(inside, 0.0, x) - total

    whole = [work[p] for p in every]
    rows = [x[:8] for x in whole]
    for q in range(B // 8):
        base = 8 * q
        within = lane - half - base
        inside = jnp.logical_and(within >= 0, within < 8)
        within_all = lane_all - half_all - base
        inside_all = jnp.logical_and(within_all >= 0, within_all < 8)
        at = [half + base + j for j in range(8)]
        cols = [gather(r, at) for r in rows]
        more = q + 1 < B // 8
        if more:
            after = [x[base + 8 : base + 16] for x in whole]
            after_cols = [gather(x, at) for x in after]
        rows = [jnp.where(inside, jnp.where(within == sub, 1.0, 0.0), r) for r in rows]
        scale = [none for _ in every]
        for j in range(8):
            mine = sub == j
            for p in every:
                g = cols[p]
                inverse = 1.0 / row_of(g[j], j)
                ratio = jnp.where(mine, 0.0, g[j]) * inverse
                scale[p] = jnp.where(mine, inverse, scale[p])
                for c in range(j + 1, 8):
                    g[c] = g[c] - ratio * row_of(g[c], j)
                rows[p] = rows[p] - ratio * row_of(rows[p], j)
        for p in every:
            new = rows[p] * scale[p]
            left, right = jnp.where(low, new, 0.0), jnp.where(low, 0.0, new)
            weights = jnp.concatenate([none] * q + [left] + [none] * 7 + [right] + [none] * (7 - q), axis=0)
            rest = jnp.where(inside_all, 0.0, whole[p]) - mm(jnp.where(inside_all, whole[p], 0.0), weights)
            parts = ([rest[:base]] if q else []) + [new] + ([rest[base + 8 :]] if more else [])
            whole[p] = jnp.concatenate(parts, axis=0)
            if more:
                rows[p] = less(after[p], after_cols[p], new, inside)
    for p in every:
        work[p] = whole[p]


def store_split(high, low, at, value):
    h = value.astype(BF16)
    high[at] = h
    low[at] = (value - h.astype(F32)).astype(BF16)


def apply(row, weights):
    wide = jnp.broadcast_to(row, (16, row.shape[1]))
    high = wide.astype(BF16).astype(F32)
    both = jnp.where(iota(wide.shape, 0) == 0, high, wide - high).astype(BF16)
    out = sum(jnp.dot(both, w, preferred_element_type=F32) for w in weights)
    return out[:1] + out[1:2]


def kernel(
    dims, diag_in, coup_in, weight_in, right_in, out, diag, coup, weight, right, in_sem,
    dch, pch, vec, in_d13, in_p10, in_d20, in_p23, in_vec, work, uq_s, et_s, xy_s,
    w1h, w1l, w2h, w2l, w3h, w3l, basis, edge_in, wbuf, wline, plane_w, note, notes, ahead, mine, theirs, sums, sums_in,
    gat_send, gat_recv, edge_send, edge_recv, pw_send, pw_recv, note_send, note_recv, ahead_send, ahead_recv,
    part_sem, sum_send, sum_recv,
):
    nl, ns, ny = dims
    m, s = lax.axis_index("lines"), lax.axis_index("seg")
    core, y_at, z_at = lax.rem(m, 2), lax.rem(m // 2, ny), m // (2 * ny)
    nz = nl // (2 * ny)

    def line_of(seg):
        return lax.rem(lax.rem((seg + 1) // 2, 2) + m, 2)

    b = line_of(s)
    mate = s + 1 - 2 * lax.rem(s, 2)
    partner = (m, mate)
    other = (lax.rem(m - 1 + 2 * b + nl, nl), s)
    others = [lax.rem(s + d, ns) for d in range(1, ns)]

    def near(index):
        at, turned = index // 2, lax.rem(index + index // 2, 2)
        return (z_at * ny * 2 + at, (s // 2) * (3 - 2 * turned) + turned)

    def far(index):
        return ((index * ny + y_at) * 2 + core, s)

    groups = ((near, 4 * ny, (y_at * 2 + core) * 2 + b), (far, nz, z_at))
    many, rank = groups[0][1:]
    step = 2 * ny

    def shifted(place, by):
        return (lax.rem(place[0] + by + nl, nl), place[1])

    herald = shifted(near(0), step)
    sends_across = rank == 0
    peers = [(m, x) for x in others]
    for place, size, own in groups[::-1]:
        peers += [place(lax.rem(own + d, size)) for d in range(1, size)]
    peers += [other, herald]
    pairs = ((diag_in, diag), (coup_in, coup), (weight_in, weight), (right_in, right))
    loads = [pltpu.make_async_copy(src, dst, in_sem.at[i]) for i, (src, dst) in enumerate(pairs)]
    for load in loads:
        load.start()
    barrier = pltpu.get_barrier_semaphore()
    for peer in peers:
        pl.semaphore_signal(barrier, inc=1, device_id=peer, device_id_type=MESH)

    @pl.when(sends_across)
    def _():
        for i in range(many):
            pl.semaphore_signal(barrier, inc=1, device_id=shifted(near(i), -step), device_id_type=MESH)

    not_first = iota((4, 2 * B), 0) > 0
    low4 = low_lanes(4)

    def lay_out(dst, tile_of, order):
        for l in range(2):
            for k in range(B // 2):
                x = tile_of(l, pl.ds(2 * B * k, 2 * B))
                xt = swap(x)
                mate_x = jnp.concatenate([x[i : i + 1] for i in order], axis=0)
                mate_t = jnp.concatenate([xt[i : i + 1] for i in order], axis=0)
                dst[pl.ds(4 * B * l + 2 * k, 4, stride=B), :] = jnp.where(low4, x, mate_t)
                dst[pl.ds(4 * B * l + 2 * k + 1, 4, stride=B), :] = jnp.where(low4, xt, mate_x)

    def diagonal(l, cols):
        edge = coup[l, :, cols]
        before = jnp.concatenate([edge[3:], edge[:3]], axis=0)
        return diag[l, :, cols] + edge + jnp.where(not_first, before, 0.0)

    loads[0].wait()
    loads[1].wait()
    lay_out(dch, diagonal, (2, 3, 0, 1))
    pl.semaphore_wait(barrier, len(peers) + jnp.where(sends_across, many, 0))

    sends = []
    chunks = ((dch, 1, in_d13), (pch, 1, in_p10), (dch, 2, in_d20), (pch, 2, in_p23))

    def chunk_copy(i, to, slot, d):
        if i == len(chunks):
            src, dst = vec, in_vec
        else:
            array, e, dst = chunks[i]
            src = array.at[pl.ds(pl.multiple_of(4 * B * line_of(to) + B * e, B), B), :]
        return pltpu.make_async_remote_copy(
            src_ref=src,
            dst_ref=dst.at[slot],
            send_sem=gat_send.at[i, d],
            recv_sem=gat_recv.at[i, slot],
            device_id=(m, to),
            device_id_type=MESH,
        )

    def send_chunk(i):
        for d, to in enumerate(others):
            copy = chunk_copy(i, to, s, d)
            copy.start()
            sends.append(copy)

    send_chunk(0)
    lay_out(pch, lambda l, cols: coup[l, :, cols], (1, 0, 3, 2))
    send_chunk(1)
    send_chunk(3)
    loads[2].wait()
    loads[3].wait()
    vec[...] = jnp.concatenate([permuted(right[...]), permuted(weight[...])], axis=0)
    send_chunk(4)
    send_chunk(2)

    def arrived(i):
        if i == len(chunks):
            in_vec[s] = vec[...]
        else:
            array, e, dst = chunks[i]
            dst[s] = array[pl.ds(pl.multiple_of(4 * B * b + B * e, B), B), :]
        for d, origin in enumerate(others):
            chunk_copy(i, origin, origin, d).wait_recv()

    def exchange(turn, source, targets):
        copies = []
        for side, to in targets:
            copy = pltpu.make_async_remote_copy(
                src_ref=source,
                dst_ref=edge_in.at[turn, side],
                send_sem=edge_send.at[turn, side],
                recv_sem=edge_recv.at[turn, side],
                device_id=to,
                device_id_type=MESH,
            )
            copy.start()
            copies.append(copy)
            sends.append(copy)

        def finish():
            for copy in copies:
                copy.wait_recv()

        return finish

    def spread(place, size, own, source, inbox, send_sem, recv_sem):
        for d in range(1, size):
            copy = pltpu.make_async_remote_copy(
                src_ref=source,
                dst_ref=inbox.at[own],
                send_sem=send_sem.at[d],
                recv_sem=recv_sem.at[own],
                device_id=place(lax.rem(own + d, size)),
                device_id_type=MESH,
            )
            copy.start()
            sends.append(copy)
        inbox[own] = source[...]

        def finish():
            for d in range(1, size):
                origin = lax.rem(own + d, size)
                pltpu.make_async_remote_copy(
                    src_ref=source,
                    dst_ref=inbox.at[origin],
                    send_sem=send_sem.at[d],
                    recv_sem=recv_sem.at[origin],
                    device_id=place(origin),
                    device_id_type=MESH,
                ).wait_recv()

        return finish

    low = low_lanes(B)
    runs = range(ns)
    arrived(0)
    invert(in_d13, ns)
    arrived(1)
    arrived(3)
    for r in runs:
        p10, p23 = in_p10[r], in_p23[r]
        if r == ns - 1:
            p23 = jnp.where(low, p23, 0.0)
        uq = mm(block_diag(in_d13[r]), jnp.concatenate([p10, p23], axis=0))
        uq_s[r] = uq
        a1 = mm(block_diag(p10), twice(uq[:B]))
        a3 = mm(block_diag(p23), twice(uq[B:]))
        if r == 0:
            arrived(2)
        d20 = in_d20[r]
        s2 = d20 - a1[:B] - a3[:B]
        if r % 2 == 0:
            work[r // 2] = s2
        else:
            work[r // 2] = jnp.where(low, work[r // 2], swap(s2))
        et_s[r] = jnp.where(low, swap(a3[:B]), a1[:B])
        xy_s[r] = jnp.where(low, swap(p23 - a3[B:]), d20 - a1[B:])
    arrived(4)
    w_mate = jnp.concatenate([in_vec[r, pl.ds(2, 1), :] for r in runs], axis=0)
    w_own = jnp.concatenate([in_vec[r, pl.ds(3, 1), :] for r in runs], axis=0)
    wbuf[...] = w_own
    wait_weights = exchange(4, wbuf, ((1, other),))
    invert(work, ns // 2)
    zs, zts, ss = [], [], []
    eye = jnp.where(iota((B, 2 * B), 0) + B == iota((B, 2 * B), 1), 1.0, 0.0)
    for r in runs:
        pack = work[r // 2]
        i2 = pack if r % 2 == 0 else swap(pack)
        et = et_s[r]
        ft = mm(i2[:, :B], et)
        cross = mm(et.T, ft)
        xy = xy_s[r] - jnp.where(low, cross[:B], cross[B:])
        zs.append(cross[B:, :B])
        zts.append(cross[:B, B:])
        ss.append(xy)
        uq = uq_s[r]
        ui = jnp.concatenate([uq[:, :B], eye[:, B:]], axis=0)
        t1 = mm(ui, jnp.concatenate([ft, i2[:, :B]], axis=1))
        t2 = mm_nt(t1[:, 2 * B :], ui)
        q0 = jnp.where(low, 0.0, uq[:B])
        q3 = jnp.where(low, swap(uq[B:]), 0.0)
        h = t1[:, : 2 * B] + jnp.concatenate([q0, q3, jnp.zeros((B, 2 * B), F32)], axis=0)
        h = jnp.concatenate([h, eye], axis=0)
        g = t2[: 2 * B, : 2 * B] + block_diag(in_d13[r])
        g = jnp.concatenate([g, t2[2 * B :, : 2 * B], jnp.zeros((B, 2 * B), F32)], axis=0)
        g2 = jnp.concatenate([t2[:, 2 * B :], jnp.zeros((B, B), F32)], axis=0)
        g2 = jnp.concatenate([g2, jnp.zeros((4 * B, B), F32)], axis=1)
        store_split(w1h, w1l, (r, slice(None), slice(0, 2 * B)), g)
        store_split(w1h, w1l, (r, slice(None), slice(2 * B, 4 * B)), g2)
        store_split(w1h, w1l, (r, slice(None), slice(4 * B, 6 * B)), h)
        ht = h.T
        w3h[r] = jnp.zeros((4 * B, 4 * B), BF16)
        w3l[r] = jnp.zeros((4 * B, 4 * B), BF16)
        store_split(w3h, w3l, (r, slice(B * r, B * r + B)), ht[B:])
        if r < ns - 1:
            store_split(w3h, w3l, (r, slice(B * r + B, B * r + 2 * B)), ht[:B])

    def separator(r):
        own = ss[r][:, B:]
        return own if r == 0 else own + ss[r - 1][:, :B]

    s0, s1, s2, s3 = (separator(r) for r in runs)
    work[0] = jnp.concatenate([s0, s3], axis=1)
    invert(work, 1)
    j0, j3 = work[0, :, :B], work[0, :, B:]
    v0, v3 = mm(j0, zs[0]), mm(j3, zts[2])
    s1 = s1 - mm(zts[0], v0)
    s2 = s2 - mm(zs[2], v3)
    work[0] = jnp.concatenate([s1, s2], axis=1)
    invert(work, 1)
    v12, v21 = mm(work[0, :, :B], zs[1]), mm(work[0, :, B:], zts[1])
    work[0] = jnp.concatenate([s1 - mm(zs[1], v21), s2 - mm(zts[1], v12)], axis=1)
    invert(work, 1)
    e11, e22 = work[0, :, :B], work[0, :, B:]
    e12, e21 = mm(v12, e22), mm(v21, e11)
    inner = jnp.concatenate(
        [jnp.concatenate([e11, e12], axis=1), jnp.concatenate([e21, e22], axis=1)], axis=0
    )
    zero = jnp.zeros((B, B), F32)
    v = jnp.concatenate([jnp.concatenate([v0, zero], axis=1), jnp.concatenate([zero, v3], axis=1)], axis=0)
    side = mm(v, inner)
    corner = mm_nt(side, v)
    back = mm_nt(inner, v)
    rows = (
        jnp.concatenate([j0 + corner[:B, :B], side[:B], corner[:B, B:]], axis=1),
        jnp.concatenate([back[:B, :B], inner[:B], back[:B, B:]], axis=1),
        jnp.concatenate([back[B:, :B], inner[B:], back[B:, B:]], axis=1),
        jnp.concatenate([corner[B:, :B], side[B:], j3 + corner[B:, B:]], axis=1),
    )
    for r in runs:
        after = rows[r + 1] if r + 1 < ns else jnp.zeros((B, 4 * B), F32)
        store_split(w2h, w2l, (slice(2 * B * r, 2 * B * r + B),), after)
        store_split(w2h, w2l, (slice(2 * B * r + B, 2 * B * r + 2 * B),), rows[r])

    def solve(t):
        first = [apply(t[r : r + 1], (w1h[r], w1l[r])) for r in runs]
        f = jnp.concatenate([x[:, 4 * B :] for x in first], axis=1)
        u = apply(f, (w2h[...], w2l[...]))
        out = [first[r][:, : 4 * B] + apply(u, (w3h[r], w3l[r])) for r in runs]
        return jnp.concatenate(out, axis=0)

    def folded(x):
        x = jnp.sum(x, axis=0, keepdims=True)
        return x[:, : 2 * B] + x[:, 2 * B :]

    def moment(i):
        note[4 + i // 2 : 5 + i // 2, 2 * B * (i % 2) : 2 * B * (i % 2) + 2 * B] = folded(
            ys[i // 2] * ts[(i + 1) // 2]
        )

    note[7:8, 2 * B :] = jnp.zeros((1, 2 * B), F32)
    t = jnp.concatenate([in_vec[r, pl.ds(b, 1), :] for r in runs], axis=0)
    ts, ys = [t], []
    basis[4] = t
    for turn in range(4):
        ys.append(solve(ts[turn]))
        basis[turn] = ys[turn]
        if turn == 3:
            break
        arrive = exchange(turn, basis.at[turn], ((0, partner), (1, other)))
        if turn == 0:
            wline[...] = jnp.where(b == 0, w_mate, w_own)
            wait_plane = spread(near, many, rank, wline, plane_w, pw_send, pw_recv)
            wait_weights()
            w_other = jnp.where(b == 0, edge_in[4, 1], w_own)
        moment(2 * turn)
        if turn:
            moment(2 * turn - 1)
        arrive()
        ts.append(w_mate * edge_in[turn, 0] + w_other * edge_in[turn, 1])
        basis[5 + turn] = ts[turn + 1]

    note[0:4, :] = ys[3]
    moment(5)
    moment(6)
    wait_notes = spread(near, many, rank, note, notes, note_send, note_recv)

    def across(to):
        return pltpu.make_async_remote_copy(
            src_ref=note.at[...],
            dst_ref=ahead,
            send_sem=ahead_send.at[to],
            recv_sem=ahead_recv.at[0],
            device_id=shifted(near(to), -step),
            device_id_type=MESH,
        )

    @pl.when(sends_across)
    def _():
        for i in range(many):
            across(i).start()

    arrive = exchange(3, basis.at[3], ((0, partner), (1, other)))
    wait_plane()
    wait_notes()
    pltpu.make_async_remote_copy(
        src_ref=note.at[...],
        dst_ref=ahead,
        send_sem=ahead_send.at[0],
        recv_sem=ahead_recv.at[0],
        device_id=herald,
        device_id_type=MESH,
    ).wait_recv()
    last = jnp.zeros((ns, 4 * B), F32)
    total = jnp.zeros((ns, 4 * B), F32)
    for i in range(many):
        following = notes[i + 1, 0:4, :] if i + 1 < many else ahead[0:4, :]
        last = last + plane_w[i] * notes[i, 0:4, :] * following
        total = total + notes[i, 4:8, :]
    last = 2.0 * folded(last)
    for i in range(8):
        sums[pl.ds(i, 1), :] = last if i == 7 else total[i // 2 : i // 2 + 1, 2 * B * (i % 2) : 2 * B * (i % 2) + 2 * B]
    wait_sums = spread(far, nz, z_at, sums, sums_in, sum_send, sum_recv)
    arrive()
    ts.append(w_mate * edge_in[3, 0] + w_other * edge_in[3, 1])
    basis[8] = ts[4]
    for j in range(9):
        mine[pl.ds(j, 1), :] = basis[j, pl.ds(mate, 1), :]
    swap_copy = pltpu.make_async_remote_copy(
        src_ref=mine,
        dst_ref=theirs,
        send_sem=part_sem.at[0],
        recv_sem=part_sem.at[1],
        device_id=partner,
        device_id_type=MESH,
    )
    swap_copy.start()
    wait_sums()
    total = sums_in[0]
    for i in range(1, nz):
        total = total + sums_in[i]
    total = jnp.sum(total, axis=1, keepdims=True)
    moments = [total[i : i + 1] for i in range(8)]
    a = [[moments[i + j] for j in range(4)] + [-moments[i + 4]] for i in range(4)]
    for k in range(3):
        inverse = 1.0 / a[k][k]
        for i in range(k + 1, 4):
            ratio = a[i][k] * inverse
            for j in range(k + 1, 5):
                a[i][j] = a[i][j] - ratio * a[k][j]
    d = [None] * 4 + [jnp.ones((1, 1), F32)]
    for k in (3, 2, 1, 0):
        value = a[k][4]
        for j in range(k + 1, 4):
            value = value - a[k][j] * d[j]
        d[k] = value / a[k][k]
    scale = 1.0 / (d[0] + d[1] + d[2] + d[3] + d[4])
    d = [value * scale for value in d]
    c = [None, None, None, d[4]]
    for k in (2, 1, 0):
        c[k] = c[k + 1] + d[k + 1]

    def combine(part):
        x, r = c[0] * part(0), d[0] * part(4)
        for k in range(1, 4):
            x = x + c[k] * part(k)
        for k in range(1, 5):
            r = r + d[k] * part(4 + k)
        return restored(x), restored(r)

    x_mine, r_mine = combine(lambda j: basis[j, pl.ds(s, 1), :])
    swap_copy.wait()
    x_theirs, r_theirs = combine(lambda j: theirs[pl.ds(j, 1), :])
    first = b == 0
    out[pl.ds(0, 1), :] = jnp.where(first, x_mine, x_theirs)
    out[pl.ds(1, 1), :] = jnp.where(first, x_theirs, x_mine)
    out[pl.ds(2, 1), :] = jnp.where(first, r_mine, r_theirs)
    out[pl.ds(3, 1), :] = jnp.where(first, r_theirs, r_mine)
    for copy in sends:
        copy.wait_send()

    @pl.when(sends_across)
    def _():
        for i in range(many):
            across(i).wait_send()


def local(diag_blocks, couplings, cross_weight, right_side):
    nl, ns = lax.axis_size("lines"), lax.axis_size("seg")
    ny = min(4, nl // 2)
    nz, many = nl // (2 * ny), 4 * ny
    shape = jax.ShapeDtypeStruct
    block = pl.BlockSpec(memory_space=pltpu.VMEM)
    vmem, dma = pltpu.VMEM, pltpu.SemaphoreType.DMA
    out = pl.pallas_call(
        functools.partial(kernel, (nl, ns, ny)),
        out_shape=shape((4, 4 * B), F32),
        in_specs=[pl.BlockSpec(memory_space=pltpu.HBM)] * 4,
        out_specs=block,
        scratch_shapes=[
            vmem(diag_blocks.shape, F32),
            vmem(couplings.shape, F32),
            vmem(cross_weight.shape, F32),
            vmem(right_side.shape, F32),
            dma((4,)),
            vmem((8 * B, 2 * B), F32),
            vmem((8 * B, 2 * B), F32),
            vmem((4, 4 * B), F32),
            vmem((ns, B, 2 * B), F32),
            vmem((ns, B, 2 * B), F32),
            vmem((ns, B, 2 * B), F32),
            vmem((ns, B, 2 * B), F32),
            vmem((ns, 4, 4 * B), F32),
            vmem((ns // 2, B, 2 * B), F32),
            vmem((ns, 2 * B, 2 * B), F32),
            vmem((ns, B, 2 * B), F32),
            vmem((ns, B, 2 * B), F32),
            vmem((ns, 4 * B, 6 * B), BF16),
            vmem((ns, 4 * B, 6 * B), BF16),
            vmem((8 * B, 4 * B), BF16),
            vmem((8 * B, 4 * B), BF16),
            vmem((ns, 4 * B, 4 * B), BF16),
            vmem((ns, 4 * B, 4 * B), BF16),
            vmem((9, 4, 4 * B), F32),
            vmem((5, 2, 4, 4 * B), F32),
            vmem((4, 4 * B), F32),
            vmem((4, 4 * B), F32),
            vmem((many, 4, 4 * B), F32),
            vmem((8, 4 * B), F32),
            vmem((many, 8, 4 * B), F32),
            vmem((8, 4 * B), F32),
            vmem((16, 4 * B), F32),
            vmem((16, 4 * B), F32),
            vmem((8, 2 * B), F32),
            vmem((nz, 8, 2 * B), F32),
            dma((5, ns)),
            dma((5, ns)),
            dma((5, 2)),
            dma((5, 2)),
            dma((many,)),
            dma((many,)),
            dma((many,)),
            dma((many,)),
            dma((many,)),
            dma((1,)),
            dma((2,)),
            dma((nz,)),
            dma((nz,)),
        ],
        compiler_params=pltpu.CompilerParams(
            collective_id=0, has_side_effects=True
        ),
        name="line_cg",
    )(diag_blocks, couplings, cross_weight, right_side)
    return out[:2], out[2:]


def solution(mesh):
    return jax.shard_map(
        local,
        mesh=mesh,
        in_specs=(
            P("lines", "seg", None),
            P("lines", "seg", None),
            P("lines", "seg"),
            P("lines", "seg"),
        ),
        out_specs=(P("lines", "seg"), P("lines", "seg")),
        check_vma=False,
    )
```

```python
import functools

import jax
import jax.numpy as jnp
from jax import lax
from jax.experimental import pallas as pl
from jax.experimental.pallas import tpu as pltpu
from jax.sharding import PartitionSpec as P

B = 64
F32 = jnp.float32
BF16 = jnp.bfloat16
MESH = pl.DeviceIdType.MESH
EXACT = lax.Precision.HIGHEST


def mm(a, b):
    return jnp.dot(a, b, precision=EXACT, preferred_element_type=F32)


def mm_nt(a, b):
    return lax.dot_general(a, b, (((1,), (1,)), ((), ())), precision=EXACT, preferred_element_type=F32)


def iota(shape, dim):
    return lax.broadcasted_iota(jnp.int32, shape, dim)


def low_lanes(rows):
    return iota((rows, 2 * B), 1) < B


def swap(x):
    return jnp.concatenate([x[:, B:], x[:, :B]], axis=1)


def block_diag(pack):
    low = low_lanes(B)
    return jnp.concatenate([jnp.where(low, pack, 0.0), jnp.where(low, 0.0, pack)], axis=0)


def twice(x):
    return jnp.concatenate([x, x], axis=0)


def permuted(x):
    return jnp.concatenate([x[:, B : 2 * B], x[:, 3 * B :], x[:, 2 * B : 3 * B], x[:, :B]], axis=1)


def restored(x):
    return jnp.concatenate([x[:, 3 * B :], x[:, :B], x[:, 2 * B : 3 * B], x[:, B : 2 * B]], axis=1)


def row_of(x, j):
    return jnp.broadcast_to(x[j : j + 1], x.shape)


def invert(work, packs, beside=iter(())):
    shape = (8, 2 * B)
    sub, lane = iota(shape, 0), iota(shape, 1)
    low = lane < B
    half = jnp.where(low, 0, B)
    lane_all = iota((B, 2 * B), 1)
    half_all = jnp.where(lane_all < B, 0, B)
    none = jnp.zeros(shape, F32)
    every = range(packs)

    def gather(x, at):
        return [jnp.take_along_axis(x, i, axis=1, mode="promise_in_bounds") for i in at]

    def less(x, x_cols, new, inside):
        c = [x_cols[j] * row_of(new, j) for j in range(8)]
        total = ((c[0] + c[1]) + (c[2] + c[3])) + ((c[4] + c[5]) + (c[6] + c[7]))
        return jnp.where(inside, 0.0, x) - total

    whole = [work[p] for p in every]
    rows = [x[:8] for x in whole]
    for q in range(B // 8):
        next(beside, None)
        base = 8 * q
        within = lane - half - base
        inside = jnp.logical_and(within >= 0, within < 8)
        within_all = lane_all - half_all - base
        inside_all = jnp.logical_and(within_all >= 0, within_all < 8)
        at = [half + base + j for j in range(8)]
        cols = [gather(r, at) for r in rows]
        more = q + 1 < B // 8
        if more:
            after = [x[base + 8 : base + 16] for x in whole]
            after_cols = [gather(x, at) for x in after]
        rows = [jnp.where(inside, jnp.where(within == sub, 1.0, 0.0), r) for r in rows]
        scale = [none for _ in every]
        for j in range(8):
            mine = sub == j
            for p in every:
                g = cols[p]
                inverse = 1.0 / row_of(g[j], j)
                ratio = jnp.where(mine, 0.0, g[j]) * inverse
                scale[p] = jnp.where(mine, inverse, scale[p])
                for c in range(j + 1, 8):
                    g[c] = g[c] - ratio * row_of(g[c], j)
                rows[p] = rows[p] - ratio * row_of(rows[p], j)
        for p in every:
            new = rows[p] * scale[p]
            left, right = jnp.where(low, new, 0.0), jnp.where(low, 0.0, new)
            weights = jnp.concatenate([none] * q + [left] + [none] * 7 + [right] + [none] * (7 - q), axis=0)
            rest = jnp.where(inside_all, 0.0, whole[p]) - mm(jnp.where(inside_all, whole[p], 0.0), weights)
            parts = ([rest[:base]] if q else []) + [new] + ([rest[base + 8 :]] if more else [])
            whole[p] = jnp.concatenate(parts, axis=0)
            if more:
                rows[p] = less(after[p], after_cols[p], new, inside)
    for p in every:
        work[p] = whole[p]


def store_split(high, low, at, value):
    h = value.astype(BF16)
    high[at] = h
    low[at] = (value - h.astype(F32)).astype(BF16)


def apply(row, weights):
    wide = jnp.broadcast_to(row, (16, row.shape[1]))
    high = wide.astype(BF16).astype(F32)
    both = jnp.where(iota(wide.shape, 0) == 0, high, wide - high).astype(BF16)
    out = sum(jnp.dot(both, w, preferred_element_type=F32) for w in weights)
    return out[:1] + out[1:2]


def kernel(
    dims, diag_in, coup_in, weight_in, right_in, out, diag, coup, weight, right, in_sem,
    dch, pch, vec, in_d13, in_p10, in_d20, in_p23, in_vec, work, uq_s, et_s, xy_s,
    w1h, w1l, w2h, w2l, w3h, w3l, basis, edge_in, wbuf, wline, plane_w, note, notes, ahead, mine, theirs, sums, sums_in,
    gat_send, gat_recv, edge_send, edge_recv, pw_send, pw_recv, note_send, note_recv, ahead_send, ahead_recv,
    part_sem, sum_send, sum_recv,
):
    nl, ns, ny = dims
    m, s = lax.axis_index("lines"), lax.axis_index("seg")
    core, y_at, z_at = lax.rem(m, 2), lax.rem(m // 2, ny), m // (2 * ny)
    nz = nl // (2 * ny)

    def line_of(seg):
        return lax.rem(lax.rem((seg + 1) // 2, 2) + m, 2)

    b = line_of(s)
    mate = s + 1 - 2 * lax.rem(s, 2)
    partner = (m, mate)
    other = (lax.rem(m - 1 + 2 * b + nl, nl), s)
    others = [lax.rem(s + d, ns) for d in range(1, ns)]

    def near(index):
        at, turned = index // 2, lax.rem(index + index // 2, 2)
        return (z_at * ny * 2 + at, (s // 2) * (3 - 2 * turned) + turned)

    def far(index):
        return ((index * ny + y_at) * 2 + core, s)

    groups = ((near, 4 * ny, (y_at * 2 + core) * 2 + b), (far, nz, z_at))
    many, rank = groups[0][1:]
    step = 2 * ny

    def shifted(place, by):
        return (lax.rem(place[0] + by + nl, nl), place[1])

    herald = shifted(near(0), step)
    sends_across = rank == 0
    peers = [(m, x) for x in others]
    for place, size, own in groups[::-1]:
        peers += [place(lax.rem(own + d, size)) for d in range(1, size)]
    peers += [other, herald]
    pairs = ((diag_in, diag), (coup_in, coup), (weight_in, weight), (right_in, right))
    loads = [pltpu.make_async_copy(src, dst, in_sem.at[i]) for i, (src, dst) in enumerate(pairs)]
    barrier = pltpu.get_barrier_semaphore()
    for peer in peers:
        pl.semaphore_signal(barrier, inc=1, device_id=peer, device_id_type=MESH)

    for load in loads:
        load.start()

    @pl.when(sends_across)
    def _():
        for i in range(many):
            pl.semaphore_signal(barrier, inc=1, device_id=shifted(near(i), -step), device_id_type=MESH)

    not_first = iota((4, 2 * B), 0) > 0
    low4 = low_lanes(4)

    def lay_out(dst, tile_of, order):
        for l in range(2):
            for k in range(B // 2):
                x = tile_of(l, pl.ds(2 * B * k, 2 * B))
                xt = swap(x)
                mate_x = jnp.concatenate([x[i : i + 1] for i in order], axis=0)
                mate_t = jnp.concatenate([xt[i : i + 1] for i in order], axis=0)
                dst[pl.ds(4 * B * l + 2 * k, 4, stride=B), :] = jnp.where(low4, x, mate_t)
                dst[pl.ds(4 * B * l + 2 * k + 1, 4, stride=B), :] = jnp.where(low4, xt, mate_x)

    def diagonal(l, cols):
        edge = coup[l, :, cols]
        before = jnp.concatenate([edge[3:], edge[:3]], axis=0)
        return diag[l, :, cols] + edge + jnp.where(not_first, before, 0.0)

    loads[0].wait()
    loads[1].wait()
    lay_out(dch, diagonal, (2, 3, 0, 1))
    pl.semaphore_wait(barrier, len(peers) + jnp.where(sends_across, many, 0))

    sends = []
    chunks = ((dch, 1, in_d13), (pch, 1, in_p10), (dch, 2, in_d20), (pch, 2, in_p23))

    def chunk_copy(i, to, slot, d):
        if i == len(chunks):
            src, dst = vec, in_vec
        else:
            array, e, dst = chunks[i]
            src = array.at[pl.ds(pl.multiple_of(4 * B * line_of(to) + B * e, B), B), :]
        return pltpu.make_async_remote_copy(
            src_ref=src,
            dst_ref=dst.at[slot],
            send_sem=gat_send.at[i, d],
            recv_sem=gat_recv.at[i, slot],
            device_id=(m, to),
            device_id_type=MESH,
        )

    def send_chunk(i):
        for d, to in enumerate(others):
            copy = chunk_copy(i, to, s, d)
            copy.start()
            sends.append(copy)

    send_chunk(0)
    lay_out(pch, lambda l, cols: coup[l, :, cols], (1, 0, 3, 2))
    send_chunk(1)
    send_chunk(3)
    loads[2].wait()
    loads[3].wait()
    vec[...] = jnp.concatenate([permuted(right[...]), permuted(weight[...])], axis=0)
    send_chunk(4)
    send_chunk(2)

    def arrived(i):
        if i == len(chunks):
            in_vec[s] = vec[...]
        else:
            array, e, dst = chunks[i]
            dst[s] = array[pl.ds(pl.multiple_of(4 * B * b + B * e, B), B), :]
        for d, origin in enumerate(others):
            chunk_copy(i, origin, origin, d).wait_recv()

    def exchange(turn, source, targets):
        copies = []
        for side, to in targets:
            copy = pltpu.make_async_remote_copy(
                src_ref=source,
                dst_ref=edge_in.at[turn, side],
                send_sem=edge_send.at[turn, side],
                recv_sem=edge_recv.at[turn, side],
                device_id=to,
                device_id_type=MESH,
            )
            copy.start()
            copies.append(copy)
            sends.append(copy)

        def finish():
            for copy in copies:
                copy.wait_recv()

        return finish

    def spread(place, size, own, source, inbox, send_sem, recv_sem):
        for d in range(1, size):
            copy = pltpu.make_async_remote_copy(
                src_ref=source,
                dst_ref=inbox.at[own],
                send_sem=send_sem.at[d],
                recv_sem=recv_sem.at[own],
                device_id=place(lax.rem(own + d, size)),
                device_id_type=MESH,
            )
            copy.start()
            sends.append(copy)
        inbox[own] = source[...]

        def finish():
            for d in range(1, size):
                origin = lax.rem(own + d, size)
                pltpu.make_async_remote_copy(
                    src_ref=source,
                    dst_ref=inbox.at[origin],
                    send_sem=send_sem.at[d],
                    recv_sem=recv_sem.at[origin],
                    device_id=place(origin),
                    device_id_type=MESH,
                ).wait_recv()

        return finish

    low = low_lanes(B)
    runs = range(ns)
    arrived(0)
    invert(in_d13, ns)
    arrived(1)
    arrived(3)
    for r in runs:
        p10, p23 = in_p10[r], in_p23[r]
        if r == ns - 1:
            p23 = jnp.where(low, p23, 0.0)
        uq = mm(block_diag(in_d13[r]), jnp.concatenate([p10, p23], axis=0))
        uq_s[r] = uq
        a1 = mm(block_diag(p10), twice(uq[:B]))
        a3 = mm(block_diag(p23), twice(uq[B:]))
        if r == 0:
            arrived(2)
        d20 = in_d20[r]
        s2 = d20 - a1[:B] - a3[:B]
        if r % 2 == 0:
            work[r // 2] = s2
        else:
            work[r // 2] = jnp.where(low, work[r // 2], swap(s2))
        et_s[r] = jnp.where(low, swap(a3[:B]), a1[:B])
        xy_s[r] = jnp.where(low, swap(p23 - a3[B:]), d20 - a1[B:])
    arrived(4)
    w_mate = jnp.concatenate([in_vec[r, pl.ds(2, 1), :] for r in runs], axis=0)
    w_own = jnp.concatenate([in_vec[r, pl.ds(3, 1), :] for r in runs], axis=0)
    wbuf[...] = w_own
    wait_weights = exchange(4, wbuf, ((1, other),))
    invert(work, ns // 2)
    zs, zts, ss, fts, i2s = [], [], [], [], []
    eye = jnp.where(iota((B, 2 * B), 0) + B == iota((B, 2 * B), 1), 1.0, 0.0)
    for r in runs:
        pack = work[r // 2]
        i2 = (pack if r % 2 == 0 else swap(pack))[:, :B]
        et = et_s[r]
        ft = mm(i2, et)
        cross = mm(et.T, ft)
        xy = xy_s[r] - jnp.where(low, cross[:B], cross[B:])
        zs.append(cross[B:, :B])
        zts.append(cross[:B, B:])
        ss.append(xy)
        fts.append(ft)
        i2s.append(i2)

    t = jnp.concatenate([in_vec[r, pl.ds(b, 1), :] for r in runs], axis=0)
    begun = []

    def operators():
        for r in runs:
            uq = uq_s[r]
            ui = jnp.concatenate([uq[:, :B], eye[:, B:]], axis=0)
            t1 = mm(ui, jnp.concatenate([fts[r], i2s[r]], axis=1))
            yield
            q0 = jnp.where(low, 0.0, uq[:B])
            q3 = jnp.where(low, swap(uq[B:]), 0.0)
            h = t1[:, : 2 * B] + jnp.concatenate([q0, q3, jnp.zeros((B, 2 * B), F32)], axis=0)
            h = jnp.concatenate([h, eye], axis=0)
            store_split(w1h, w1l, (r, slice(None), slice(4 * B, 6 * B)), h)
            yield
            t2 = mm_nt(t1[:, 2 * B :], ui)
            g = t2[: 2 * B, : 2 * B] + block_diag(in_d13[r])
            g = jnp.concatenate([g, t2[2 * B :, : 2 * B], jnp.zeros((B, 2 * B), F32)], axis=0)
            store_split(w1h, w1l, (r, slice(None), slice(0, 2 * B)), g)
            yield
            g = jnp.concatenate([t2[:, 2 * B :], jnp.zeros((B, B), F32)], axis=0)
            g = jnp.concatenate([g, jnp.zeros((4 * B, B), F32)], axis=1)
            store_split(w1h, w1l, (r, slice(None), slice(2 * B, 4 * B)), g)
            yield
            ht = h.T
            w3h[r] = jnp.zeros((4 * B, 4 * B), BF16)
            w3l[r] = jnp.zeros((4 * B, 4 * B), BF16)
            store_split(w3h, w3l, (r, slice(B * r, B * r + B)), ht[B:])
            if r < ns - 1:
                store_split(w3h, w3l, (r, slice(B * r + B, B * r + 2 * B)), ht[:B])
            yield
            begun.append(apply(t[r : r + 1], (w1h[r], w1l[r])))
            yield

    beside = operators()

    def separator(r):
        own = ss[r][:, B:]
        return own if r == 0 else own + ss[r - 1][:, :B]

    s0, s1, s2, s3 = (separator(r) for r in runs)
    work[0] = jnp.concatenate([s0, s3], axis=1)
    invert(work, 1, beside)
    j0, j3 = work[0, :, :B], work[0, :, B:]
    v0, v3 = mm(j0, zs[0]), mm(j3, zts[2])
    s1 = s1 - mm(zts[0], v0)
    s2 = s2 - mm(zs[2], v3)
    work[0] = jnp.concatenate([s1, s2], axis=1)
    invert(work, 1, beside)
    v12, v21 = mm(work[0, :, :B], zs[1]), mm(work[0, :, B:], zts[1])
    work[0] = jnp.concatenate([s1 - mm(zs[1], v21), s2 - mm(zts[1], v12)], axis=1)
    invert(work, 1, beside)
    for _ in beside:
        pass
    e11, e22 = work[0, :, :B], work[0, :, B:]
    e12, e21 = mm(v12, e22), mm(v21, e11)
    inner = jnp.concatenate(
        [jnp.concatenate([e11, e12], axis=1), jnp.concatenate([e21, e22], axis=1)], axis=0
    )
    zero = jnp.zeros((B, B), F32)
    v = jnp.concatenate([jnp.concatenate([v0, zero], axis=1), jnp.concatenate([zero, v3], axis=1)], axis=0)
    side = mm(v, inner)
    corner = mm_nt(side, v)
    back = mm_nt(inner, v)
    rows = (
        jnp.concatenate([j0 + corner[:B, :B], side[:B], corner[:B, B:]], axis=1),
        jnp.concatenate([back[:B, :B], inner[:B], back[:B, B:]], axis=1),
        jnp.concatenate([back[B:, :B], inner[B:], back[B:, B:]], axis=1),
        jnp.concatenate([corner[B:, :B], side[B:], j3 + corner[B:, B:]], axis=1),
    )
    for r in runs:
        after = rows[r + 1] if r + 1 < ns else jnp.zeros((B, 4 * B), F32)
        store_split(w2h, w2l, (slice(2 * B * r, 2 * B * r + B),), after)
        store_split(w2h, w2l, (slice(2 * B * r + B, 2 * B * r + 2 * B),), rows[r])

    def begin(t):
        return [apply(t[r : r + 1], (w1h[r], w1l[r])) for r in runs]

    def solve(first):
        f = jnp.concatenate([x[:, 4 * B :] for x in first], axis=1)
        u = apply(f, (w2h[...], w2l[...]))
        out = [first[r][:, : 4 * B] + apply(u, (w3h[r], w3l[r])) for r in runs]
        return jnp.concatenate(out, axis=0)

    def folded(x):
        x = jnp.sum(x, axis=0, keepdims=True)
        return x[:, : 2 * B] + x[:, 2 * B :]

    def moment(i):
        note[4 + i // 2 : 5 + i // 2, 2 * B * (i % 2) : 2 * B * (i % 2) + 2 * B] = folded(
            ys[i // 2] * ts[(i + 1) // 2]
        )

    note[7:8, 2 * B :] = jnp.zeros((1, 2 * B), F32)
    ts, ys = [t], []
    basis[4] = t
    for turn in range(4):
        ys.append(solve(begin(ts[turn]) if turn else begun))
        basis[turn] = ys[turn]
        if turn == 3:
            break
        arrive = exchange(turn, basis.at[turn], ((0, partner), (1, other)))
        if turn == 0:
            wline[...] = jnp.where(b == 0, w_mate, w_own)
            wait_plane = spread(near, many, rank, wline, plane_w, pw_send, pw_recv)
            wait_weights()
            w_other = jnp.where(b == 0, edge_in[4, 1], w_own)
        moment(2 * turn)
        if turn:
            moment(2 * turn - 1)
        arrive()
        ts.append(w_mate * edge_in[turn, 0] + w_other * edge_in[turn, 1])
        basis[5 + turn] = ts[turn + 1]

    note[0:4, :] = ys[3]
    moment(5)
    moment(6)
    wait_notes = spread(near, many, rank, note, notes, note_send, note_recv)

    def across(to):
        return pltpu.make_async_remote_copy(
            src_ref=note.at[...],
            dst_ref=ahead,
            send_sem=ahead_send.at[to],
            recv_sem=ahead_recv.at[0],
            device_id=shifted(near(to), -step),
            device_id_type=MESH,
        )

    @pl.when(sends_across)
    def _():
        for i in range(many):
            across(i).start()

    arrive = exchange(3, basis.at[3], ((0, partner), (1, other)))
    wait_plane()
    wait_notes()
    pltpu.make_async_remote_copy(
        src_ref=note.at[...],
        dst_ref=ahead,
        send_sem=ahead_send.at[0],
        recv_sem=ahead_recv.at[0],
        device_id=herald,
        device_id_type=MESH,
    ).wait_recv()
    last = jnp.zeros((ns, 4 * B), F32)
    total = jnp.zeros((ns, 4 * B), F32)
    for i in range(many):
        following = notes[i + 1, 0:4, :] if i + 1 < many else ahead[0:4, :]
        last = last + plane_w[i] * notes[i, 0:4, :] * following
        total = total + notes[i, 4:8, :]
    last = 2.0 * folded(last)
    for i in range(8):
        sums[pl.ds(i, 1), :] = last if i == 7 else total[i // 2 : i // 2 + 1, 2 * B * (i % 2) : 2 * B * (i % 2) + 2 * B]
    wait_sums = spread(far, nz, z_at, sums, sums_in, sum_send, sum_recv)
    arrive()
    ts.append(w_mate * edge_in[3, 0] + w_other * edge_in[3, 1])
    basis[8] = ts[4]
    for j in range(9):
        mine[pl.ds(j, 1), :] = basis[j, pl.ds(mate, 1), :]
    swap_copy = pltpu.make_async_remote_copy(
        src_ref=mine,
        dst_ref=theirs,
        send_sem=part_sem.at[0],
        recv_sem=part_sem.at[1],
        device_id=partner,
        device_id_type=MESH,
    )
    swap_copy.start()
    wait_sums()
    total = sums_in[0]
    for i in range(1, nz):
        total = total + sums_in[i]
    total = jnp.sum(total, axis=1, keepdims=True)
    moments = [total[i : i + 1] for i in range(8)]
    a = [[moments[i + j] for j in range(4)] + [-moments[i + 4]] for i in range(4)]
    for k in range(3):
        inverse = 1.0 / a[k][k]
        for i in range(k + 1, 4):
            ratio = a[i][k] * inverse
            for j in range(k + 1, 5):
                a[i][j] = a[i][j] - ratio * a[k][j]
    d = [None] * 4 + [jnp.ones((1, 1), F32)]
    for k in (3, 2, 1, 0):
        value = a[k][4]
        for j in range(k + 1, 4):
            value = value - a[k][j] * d[j]
        d[k] = value / a[k][k]
    scale = 1.0 / (d[0] + d[1] + d[2] + d[3] + d[4])
    d = [value * scale for value in d]
    c = [None, None, None, d[4]]
    for k in (2, 1, 0):
        c[k] = c[k + 1] + d[k + 1]

    def combine(part):
        x, r = c[0] * part(0), d[0] * part(4)
        for k in range(1, 4):
            x = x + c[k] * part(k)
        for k in range(1, 5):
            r = r + d[k] * part(4 + k)
        return restored(x), restored(r)

    x_mine, r_mine = combine(lambda j: basis[j, pl.ds(s, 1), :])
    swap_copy.wait()
    x_theirs, r_theirs = combine(lambda j: theirs[pl.ds(j, 1), :])
    first = b == 0
    out[pl.ds(0, 1), :] = jnp.where(first, x_mine, x_theirs)
    out[pl.ds(1, 1), :] = jnp.where(first, x_theirs, x_mine)
    out[pl.ds(2, 1), :] = jnp.where(first, r_mine, r_theirs)
    out[pl.ds(3, 1), :] = jnp.where(first, r_theirs, r_mine)
    for copy in sends:
        copy.wait_send()

    @pl.when(sends_across)
    def _():
        for i in range(many):
            across(i).wait_send()


def local(diag_blocks, couplings, cross_weight, right_side):
    nl, ns = lax.axis_size("lines"), lax.axis_size("seg")
    ny = min(4, nl // 2)
    nz, many = nl // (2 * ny), 4 * ny
    shape = jax.ShapeDtypeStruct
    block = pl.BlockSpec(memory_space=pltpu.VMEM)
    vmem, dma = pltpu.VMEM, pltpu.SemaphoreType.DMA
    out = pl.pallas_call(
        functools.partial(kernel, (nl, ns, ny)),
        out_shape=shape((4, 4 * B), F32),
        in_specs=[pl.BlockSpec(memory_space=pltpu.HBM)] * 4,
        out_specs=block,
        scratch_shapes=[
            vmem(diag_blocks.shape, F32),
            vmem(couplings.shape, F32),
            vmem(cross_weight.shape, F32),
            vmem(right_side.shape, F32),
            dma((4,)),
            vmem((8 * B, 2 * B), F32),
            vmem((8 * B, 2 * B), F32),
            vmem((4, 4 * B), F32),
            vmem((ns, B, 2 * B), F32),
            vmem((ns, B, 2 * B), F32),
            vmem((ns, B, 2 * B), F32),
            vmem((ns, B, 2 * B), F32),
            vmem((ns, 4, 4 * B), F32),
            vmem((ns // 2, B, 2 * B), F32),
            vmem((ns, 2 * B, 2 * B), F32),
            vmem((ns, B, 2 * B), F32),
            vmem((ns, B, 2 * B), F32),
            vmem((ns, 4 * B, 6 * B), BF16),
            vmem((ns, 4 * B, 6 * B), BF16),
            vmem((8 * B, 4 * B), BF16),
            vmem((8 * B, 4 * B), BF16),
            vmem((ns, 4 * B, 4 * B), BF16),
            vmem((ns, 4 * B, 4 * B), BF16),
            vmem((9, 4, 4 * B), F32),
            vmem((5, 2, 4, 4 * B), F32),
            vmem((4, 4 * B), F32),
            vmem((4, 4 * B), F32),
            vmem((many, 4, 4 * B), F32),
            vmem((8, 4 * B), F32),
            vmem((many, 8, 4 * B), F32),
            vmem((8, 4 * B), F32),
            vmem((16, 4 * B), F32),
            vmem((16, 4 * B), F32),
            vmem((8, 2 * B), F32),
            vmem((nz, 8, 2 * B), F32),
            dma((5, ns)),
            dma((5, ns)),
            dma((5, 2)),
            dma((5, 2)),
            dma((many,)),
            dma((many,)),
            dma((many,)),
            dma((many,)),
            dma((many,)),
            dma((1,)),
            dma((2,)),
            dma((nz,)),
            dma((nz,)),
        ],
        compiler_params=pltpu.CompilerParams(
            collective_id=0, has_side_effects=True
        ),
        name="line_cg",
    )(diag_blocks, couplings, cross_weight, right_side)
    return out[:2], out[2:]


def solution(mesh):
    return jax.shard_map(
        local,
        mesh=mesh,
        in_specs=(
            P("lines", "seg", None),
            P("lines", "seg", None),
            P("lines", "seg"),
            P("lines", "seg"),
        ),
        out_specs=(P("lines", "seg"), P("lines", "seg")),
        check_vma=False,
    )
```

```python
import functools

import jax
import jax.numpy as jnp
from jax import lax
from jax.experimental import pallas as pl
from jax.experimental.pallas import tpu as pltpu
from jax.sharding import PartitionSpec as P

B = 64
F32 = jnp.float32
BF16 = jnp.bfloat16
MESH = pl.DeviceIdType.MESH
EXACT = lax.Precision.HIGHEST


def mm(a, b):
    return jnp.dot(a, b, precision=EXACT, preferred_element_type=F32)


def mm_nt(a, b):
    return lax.dot_general(a, b, (((1,), (1,)), ((), ())), precision=EXACT, preferred_element_type=F32)


def iota(shape, dim):
    return lax.broadcasted_iota(jnp.int32, shape, dim)


def low_lanes(rows):
    return iota((rows, 2 * B), 1) < B


def swap(x):
    return jnp.concatenate([x[:, B:], x[:, :B]], axis=1)


def block_diag(pack):
    low = low_lanes(B)
    return jnp.concatenate([jnp.where(low, pack, 0.0), jnp.where(low, 0.0, pack)], axis=0)


def twice(x):
    return jnp.concatenate([x, x], axis=0)


def permuted(x):
    return jnp.concatenate([x[:, B : 2 * B], x[:, 3 * B :], x[:, 2 * B : 3 * B], x[:, :B]], axis=1)


def restored(x):
    return jnp.concatenate([x[:, 3 * B :], x[:, :B], x[:, 2 * B : 3 * B], x[:, B : 2 * B]], axis=1)


def row_of(x, j):
    return jnp.broadcast_to(x[j : j + 1], x.shape)


def invert(work, packs, beside=iter(()), tiles=1):
    shape = (8, 2 * B)
    wide = 8 * tiles
    size = work.shape[1]
    paired = size == B
    sub, lane = iota(shape, 0), iota(shape, 1)
    low = lane < B
    lane_all = iota((size, 2 * B), 1)
    half = jnp.where(low, 0, B) if paired else jnp.zeros_like(lane)
    half_all = jnp.where(lane_all < B, 0, B) if paired else jnp.zeros_like(lane_all)
    none = jnp.zeros(shape, F32)
    every, each = range(packs), range(tiles)

    def gather(x, at):
        return [jnp.take_along_axis(x, i, axis=1, mode="promise_in_bounds") for i in at]

    def total(terms):
        while len(terms) > 1:
            terms = [x + y for x, y in zip(terms[::2], terms[1::2])]
        return terms[0]

    def cut(x, base):
        return [x[base + 8 * t : base + 8 * t + 8] for t in each]

    whole = [work[p] for p in every]
    rows = [cut(x, 0) for x in whole]
    for q in range(size // wide):
        for _ in each:
            next(beside, None)
        base = wide * q
        within = lane - half - base
        inside = jnp.logical_and(within >= 0, within < wide)
        within_all = lane_all - half_all - base
        inside_all = jnp.logical_and(within_all >= 0, within_all < wide)
        at = [half + base + j for j in range(wide)]
        cols = [[gather(x, at) for x in r] for r in rows]
        more = base + wide < size
        if more:
            after = [cut(x, base + wide) for x in whole]
            after_cols = [[gather(x, at) for x in r] for r in after]
        rows = [[jnp.where(inside, jnp.where(within == sub + 8 * t, 1.0, 0.0), r[t]) for t in each] for r in rows]
        scale = [[none for _ in each] for _ in every]
        for j in range(wide):
            own, at_row = j // 8, j % 8
            mine = sub == at_row
            for p in every:
                g = cols[p]
                inverse = 1.0 / row_of(g[own][j], at_row)
                ratio = [(jnp.where(mine, 0.0, g[t][j]) if t == own else g[t][j]) * inverse for t in each]
                scale[p][own] = jnp.where(mine, inverse, scale[p][own])
                for c in range(j + 1, wide):
                    pivot = row_of(g[own][c], at_row)
                    for t in each:
                        g[t][c] = g[t][c] - ratio[t] * pivot
                pivot = row_of(rows[p][own], at_row)
                rows[p] = [rows[p][t] - ratio[t] * pivot for t in each]
        for p in every:
            new = [rows[p][t] * scale[p][t] for t in each]
            before, behind = [none] * (base // 8), [none] * ((size - base) // 8 - tiles)
            placed = before + new + behind
            if paired:
                left = before + [jnp.where(low, x, 0.0) for x in new] + behind
                placed = left + before + [jnp.where(low, 0.0, x) for x in new] + behind
            weights = jnp.concatenate(placed, axis=0)
            rest = jnp.where(inside_all, 0.0, whole[p]) - mm(jnp.where(inside_all, whole[p], 0.0), weights)
            parts = ([rest[:base]] if q else []) + new + ([rest[base + wide :]] if more else [])
            whole[p] = jnp.concatenate(parts, axis=0)
            if more:
                spread_rows = [row_of(new[j // 8], j % 8) for j in range(wide)]
                rows[p] = [
                    jnp.where(inside, 0.0, after[p][t])
                    - total([x * y for x, y in zip(after_cols[p][t], spread_rows)])
                    for t in each
                ]
    for p in every:
        work[p] = whole[p]


def store_split(high, low, at, value):
    h = value.astype(BF16)
    high[at] = h
    low[at] = (value - h.astype(F32)).astype(BF16)


def apply(row, weights):
    wide = jnp.broadcast_to(row, (16, row.shape[1]))
    high = wide.astype(BF16).astype(F32)
    both = jnp.where(iota(wide.shape, 0) == 0, high, wide - high).astype(BF16)
    out = sum(jnp.dot(both, w, preferred_element_type=F32) for w in weights)
    return out[:1] + out[1:2]


def kernel(
    dims, diag_in, coup_in, weight_in, right_in, out, diag, coup, weight, right, in_sem,
    dch, pch, vec, in_d13, in_p10, in_d20, in_p23, in_vec, work, middle, uq_s, et_s, xy_s,
    w1h, w1l, w2h, w2l, w3h, w3l, basis, edge_in, wbuf, wline, plane_w, note, notes, ahead, mine, theirs, sums, sums_in,
    gat_send, gat_recv, edge_send, edge_recv, pw_send, pw_recv, note_send, note_recv, ahead_send, ahead_recv,
    part_sem, sum_send, sum_recv,
):
    nl, ns, ny = dims
    m, s = lax.axis_index("lines"), lax.axis_index("seg")
    core, y_at, z_at = lax.rem(m, 2), lax.rem(m // 2, ny), m // (2 * ny)
    nz = nl // (2 * ny)

    def line_of(seg):
        return lax.rem(lax.rem((seg + 1) // 2, 2) + m, 2)

    b = line_of(s)
    mate = s + 1 - 2 * lax.rem(s, 2)
    partner = (m, mate)
    other = (lax.rem(m - 1 + 2 * b + nl, nl), s)
    others = [lax.rem(s + d, ns) for d in range(1, ns)]

    def near(index):
        at, turned = index // 2, lax.rem(index + index // 2, 2)
        return (z_at * ny * 2 + at, (s // 2) * (3 - 2 * turned) + turned)

    def far(index):
        return ((index * ny + y_at) * 2 + core, s)

    groups = ((near, 4 * ny, (y_at * 2 + core) * 2 + b), (far, nz, z_at))
    many, rank = groups[0][1:]
    step = 2 * ny

    def shifted(place, by):
        return (lax.rem(place[0] + by + nl, nl), place[1])

    herald = shifted(near(0), step)
    sends_across = rank == 0
    peers = [(m, x) for x in others]
    for place, size, own in groups[::-1]:
        peers += [place(lax.rem(own + d, size)) for d in range(1, size)]
    peers += [other, herald]
    pairs = ((diag_in, diag), (coup_in, coup), (weight_in, weight), (right_in, right))
    loads = [pltpu.make_async_copy(src, dst, in_sem.at[i]) for i, (src, dst) in enumerate(pairs)]
    barrier = pltpu.get_barrier_semaphore()
    for peer in peers:
        pl.semaphore_signal(barrier, inc=1, device_id=peer, device_id_type=MESH)

    for load in loads:
        load.start()

    @pl.when(sends_across)
    def _():
        for i in range(many):
            pl.semaphore_signal(barrier, inc=1, device_id=shifted(near(i), -step), device_id_type=MESH)

    not_first = iota((4, 2 * B), 0) > 0
    low4 = low_lanes(4)

    def lay_out(dst, tile_of, order):
        for l in range(2):
            for k in range(B // 2):
                x = tile_of(l, pl.ds(2 * B * k, 2 * B))
                xt = swap(x)
                mate_x = jnp.concatenate([x[i : i + 1] for i in order], axis=0)
                mate_t = jnp.concatenate([xt[i : i + 1] for i in order], axis=0)
                dst[pl.ds(4 * B * l + 2 * k, 4, stride=B), :] = jnp.where(low4, x, mate_t)
                dst[pl.ds(4 * B * l + 2 * k + 1, 4, stride=B), :] = jnp.where(low4, xt, mate_x)

    def diagonal(l, cols):
        edge = coup[l, :, cols]
        before = jnp.concatenate([edge[3:], edge[:3]], axis=0)
        return diag[l, :, cols] + edge + jnp.where(not_first, before, 0.0)

    loads[0].wait()
    loads[1].wait()
    lay_out(dch, diagonal, (2, 3, 0, 1))
    pl.semaphore_wait(barrier, len(peers) + jnp.where(sends_across, many, 0))

    sends = []
    chunks = ((dch, 1, in_d13), (pch, 1, in_p10), (dch, 2, in_d20), (pch, 2, in_p23))

    def chunk_copy(i, to, slot, d):
        if i == len(chunks):
            src, dst = vec, in_vec
        else:
            array, e, dst = chunks[i]
            src = array.at[pl.ds(pl.multiple_of(4 * B * line_of(to) + B * e, B), B), :]
        return pltpu.make_async_remote_copy(
            src_ref=src,
            dst_ref=dst.at[slot],
            send_sem=gat_send.at[i, d],
            recv_sem=gat_recv.at[i, slot],
            device_id=(m, to),
            device_id_type=MESH,
        )

    def send_chunk(i):
        for d, to in enumerate(others):
            copy = chunk_copy(i, to, s, d)
            copy.start()
            sends.append(copy)

    send_chunk(0)
    lay_out(pch, lambda l, cols: coup[l, :, cols], (1, 0, 3, 2))
    send_chunk(1)
    send_chunk(3)
    loads[2].wait()
    loads[3].wait()
    vec[...] = jnp.concatenate([permuted(right[...]), permuted(weight[...])], axis=0)
    send_chunk(4)
    send_chunk(2)

    def arrived(i):
        if i == len(chunks):
            in_vec[s] = vec[...]
        else:
            array, e, dst = chunks[i]
            dst[s] = array[pl.ds(pl.multiple_of(4 * B * b + B * e, B), B), :]
        for d, origin in enumerate(others):
            chunk_copy(i, origin, origin, d).wait_recv()

    def exchange(turn, source, targets):
        copies = []
        for side, to in targets:
            copy = pltpu.make_async_remote_copy(
                src_ref=source,
                dst_ref=edge_in.at[turn, side],
                send_sem=edge_send.at[turn, side],
                recv_sem=edge_recv.at[turn, side],
                device_id=to,
                device_id_type=MESH,
            )
            copy.start()
            copies.append(copy)
            sends.append(copy)

        def finish():
            for copy in copies:
                copy.wait_recv()

        return finish

    def spread(place, size, own, source, inbox, send_sem, recv_sem):
        for d in range(1, size):
            copy = pltpu.make_async_remote_copy(
                src_ref=source,
                dst_ref=inbox.at[own],
                send_sem=send_sem.at[d],
                recv_sem=recv_sem.at[own],
                device_id=place(lax.rem(own + d, size)),
                device_id_type=MESH,
            )
            copy.start()
            sends.append(copy)
        inbox[own] = source[...]

        def finish():
            for d in range(1, size):
                origin = lax.rem(own + d, size)
                pltpu.make_async_remote_copy(
                    src_ref=source,
                    dst_ref=inbox.at[origin],
                    send_sem=send_sem.at[d],
                    recv_sem=recv_sem.at[origin],
                    device_id=place(origin),
                    device_id_type=MESH,
                ).wait_recv()

        return finish

    low = low_lanes(B)
    runs = range(ns)
    arrived(0)
    invert(in_d13, ns)
    arrived(1)
    arrived(3)
    for r in runs:
        p10, p23 = in_p10[r], in_p23[r]
        if r == ns - 1:
            p23 = jnp.where(low, p23, 0.0)
        uq = mm(block_diag(in_d13[r]), jnp.concatenate([p10, p23], axis=0))
        uq_s[r] = uq
        a1 = mm(block_diag(p10), twice(uq[:B]))
        a3 = mm(block_diag(p23), twice(uq[B:]))
        if r == 0:
            arrived(2)
        d20 = in_d20[r]
        s2 = d20 - a1[:B] - a3[:B]
        if r % 2 == 0:
            work[r // 2] = s2
        else:
            work[r // 2] = jnp.where(low, work[r // 2], swap(s2))
        et_s[r] = jnp.where(low, swap(a3[:B]), a1[:B])
        xy_s[r] = jnp.where(low, swap(p23 - a3[B:]), d20 - a1[B:])
    arrived(4)
    w_mate = jnp.concatenate([in_vec[r, pl.ds(2, 1), :] for r in runs], axis=0)
    w_own = jnp.concatenate([in_vec[r, pl.ds(3, 1), :] for r in runs], axis=0)
    wbuf[...] = w_own
    wait_weights = exchange(4, wbuf, ((1, other),))
    invert(work, ns // 2)
    zs, zts, ss, fts, i2s = [], [], [], [], []
    eye = jnp.where(iota((B, 2 * B), 0) + B == iota((B, 2 * B), 1), 1.0, 0.0)
    for r in runs:
        pack = work[r // 2]
        i2 = (pack if r % 2 == 0 else swap(pack))[:, :B]
        et = et_s[r]
        ft = mm(i2, et)
        cross = mm(et.T, ft)
        xy = xy_s[r] - jnp.where(low, cross[:B], cross[B:])
        zs.append(cross[B:, :B])
        zts.append(cross[:B, B:])
        ss.append(xy)
        fts.append(ft)
        i2s.append(i2)

    t = jnp.concatenate([in_vec[r, pl.ds(b, 1), :] for r in runs], axis=0)
    begun = []

    def operators():
        for r in runs:
            uq = uq_s[r]
            ui = jnp.concatenate([uq[:, :B], eye[:, B:]], axis=0)
            t1 = mm(ui, jnp.concatenate([fts[r], i2s[r]], axis=1))
            yield
            q0 = jnp.where(low, 0.0, uq[:B])
            q3 = jnp.where(low, swap(uq[B:]), 0.0)
            h = t1[:, : 2 * B] + jnp.concatenate([q0, q3, jnp.zeros((B, 2 * B), F32)], axis=0)
            h = jnp.concatenate([h, eye], axis=0)
            store_split(w1h, w1l, (r, slice(None), slice(4 * B, 6 * B)), h)
            yield
            t2 = mm_nt(t1[:, 2 * B :], ui)
            g = t2[: 2 * B, : 2 * B] + block_diag(in_d13[r])
            g = jnp.concatenate([g, t2[2 * B :, : 2 * B], jnp.zeros((B, 2 * B), F32)], axis=0)
            store_split(w1h, w1l, (r, slice(None), slice(0, 2 * B)), g)
            yield
            g = jnp.concatenate([t2[:, 2 * B :], jnp.zeros((B, B), F32)], axis=0)
            g = jnp.concatenate([g, jnp.zeros((4 * B, B), F32)], axis=1)
            store_split(w1h, w1l, (r, slice(None), slice(2 * B, 4 * B)), g)
            yield
            ht = h.T
            w3h[r] = jnp.zeros((4 * B, 4 * B), BF16)
            w3l[r] = jnp.zeros((4 * B, 4 * B), BF16)
            store_split(w3h, w3l, (r, slice(B * r, B * r + B)), ht[B:])
            if r < ns - 1:
                store_split(w3h, w3l, (r, slice(B * r + B, B * r + 2 * B)), ht[:B])
            yield
            begun.append(apply(t[r : r + 1], (w1h[r], w1l[r])))
            yield

    beside = operators()

    def separator(r):
        own = ss[r][:, B:]
        return own if r == 0 else own + ss[r - 1][:, :B]

    s0, s1, s2, s3 = (separator(r) for r in runs)
    work[0] = jnp.concatenate([s0, s3], axis=1)
    invert(work, 1, beside, 2)
    j0, j3 = work[0, :, :B], work[0, :, B:]
    v0, v3 = mm(j0, zs[0]), mm(j3, zts[2])
    s1 = s1 - mm(zts[0], v0)
    s2 = s2 - mm(zs[2], v3)
    middle[0, :B, :] = jnp.concatenate([s1, -zs[1]], axis=1)
    middle[0, B:, :] = jnp.concatenate([-zts[1], s2], axis=1)
    invert(middle, 1, beside, 2)
    for _ in beside:
        pass
    inner = middle[0]
    zero = jnp.zeros((B, B), F32)
    v = jnp.concatenate([jnp.concatenate([v0, zero], axis=1), jnp.concatenate([zero, v3], axis=1)], axis=0)
    side = mm(v, inner)
    corner = mm_nt(side, v)
    back = mm_nt(inner, v)
    rows = (
        jnp.concatenate([j0 + corner[:B, :B], side[:B], corner[:B, B:]], axis=1),
        jnp.concatenate([back[:B, :B], inner[:B], back[:B, B:]], axis=1),
        jnp.concatenate([back[B:, :B], inner[B:], back[B:, B:]], axis=1),
        jnp.concatenate([corner[B:, :B], side[B:], j3 + corner[B:, B:]], axis=1),
    )
    for r in runs:
        after = rows[r + 1] if r + 1 < ns else jnp.zeros((B, 4 * B), F32)
        store_split(w2h, w2l, (slice(2 * B * r, 2 * B * r + B),), after)
        store_split(w2h, w2l, (slice(2 * B * r + B, 2 * B * r + 2 * B),), rows[r])

    def begin(t):
        return [apply(t[r : r + 1], (w1h[r], w1l[r])) for r in runs]

    def solve(first):
        f = jnp.concatenate([x[:, 4 * B :] for x in first], axis=1)
        u = apply(f, (w2h[...], w2l[...]))
        out = [first[r][:, : 4 * B] + apply(u, (w3h[r], w3l[r])) for r in runs]
        return jnp.concatenate(out, axis=0)

    def folded(x):
        x = jnp.sum(x, axis=0, keepdims=True)
        return x[:, : 2 * B] + x[:, 2 * B :]

    def moment(i):
        note[4 + i // 2 : 5 + i // 2, 2 * B * (i % 2) : 2 * B * (i % 2) + 2 * B] = folded(
            ys[i // 2] * ts[(i + 1) // 2]
        )

    note[7:8, 2 * B :] = jnp.zeros((1, 2 * B), F32)
    ts, ys = [t], []
    basis[4] = t
    for turn in range(4):
        ys.append(solve(begin(ts[turn]) if turn else begun))
        basis[turn] = ys[turn]
        if turn == 3:
            break
        arrive = exchange(turn, basis.at[turn], ((0, partner), (1, other)))
        if turn == 0:
            wline[...] = jnp.where(b == 0, w_mate, w_own)
            wait_plane = spread(near, many, rank, wline, plane_w, pw_send, pw_recv)
            wait_weights()
            w_other = jnp.where(b == 0, edge_in[4, 1], w_own)
        moment(2 * turn)
        if turn:
            moment(2 * turn - 1)
        arrive()
        ts.append(w_mate * edge_in[turn, 0] + w_other * edge_in[turn, 1])
        basis[5 + turn] = ts[turn + 1]

    note[0:4, :] = ys[3]
    moment(5)
    moment(6)
    wait_notes = spread(near, many, rank, note, notes, note_send, note_recv)

    def across(to):
        return pltpu.make_async_remote_copy(
            src_ref=note.at[...],
            dst_ref=ahead,
            send_sem=ahead_send.at[to],
            recv_sem=ahead_recv.at[0],
            device_id=shifted(near(to), -step),
            device_id_type=MESH,
        )

    @pl.when(sends_across)
    def _():
        for i in range(many):
            across(i).start()

    arrive = exchange(3, basis.at[3], ((0, partner), (1, other)))
    wait_plane()
    wait_notes()
    pltpu.make_async_remote_copy(
        src_ref=note.at[...],
        dst_ref=ahead,
        send_sem=ahead_send.at[0],
        recv_sem=ahead_recv.at[0],
        device_id=herald,
        device_id_type=MESH,
    ).wait_recv()
    last = jnp.zeros((ns, 4 * B), F32)
    total = jnp.zeros((ns, 4 * B), F32)
    for i in range(many):
        following = notes[i + 1, 0:4, :] if i + 1 < many else ahead[0:4, :]
        last = last + plane_w[i] * notes[i, 0:4, :] * following
        total = total + notes[i, 4:8, :]
    last = 2.0 * folded(last)
    for i in range(8):
        sums[pl.ds(i, 1), :] = last if i == 7 else total[i // 2 : i // 2 + 1, 2 * B * (i % 2) : 2 * B * (i % 2) + 2 * B]
    wait_sums = spread(far, nz, z_at, sums, sums_in, sum_send, sum_recv)
    arrive()
    ts.append(w_mate * edge_in[3, 0] + w_other * edge_in[3, 1])
    basis[8] = ts[4]
    for j in range(9):
        mine[pl.ds(j, 1), :] = basis[j, pl.ds(mate, 1), :]
    swap_copy = pltpu.make_async_remote_copy(
        src_ref=mine,
        dst_ref=theirs,
        send_sem=part_sem.at[0],
        recv_sem=part_sem.at[1],
        device_id=partner,
        device_id_type=MESH,
    )
    swap_copy.start()
    wait_sums()
    total = sums_in[0]
    for i in range(1, nz):
        total = total + sums_in[i]
    total = jnp.sum(total, axis=1, keepdims=True)
    moments = [total[i : i + 1] for i in range(8)]
    a = [[moments[i + j] for j in range(4)] + [-moments[i + 4]] for i in range(4)]
    for k in range(3):
        inverse = 1.0 / a[k][k]
        for i in range(k + 1, 4):
            ratio = a[i][k] * inverse
            for j in range(k + 1, 5):
                a[i][j] = a[i][j] - ratio * a[k][j]
    d = [None] * 4 + [jnp.ones((1, 1), F32)]
    for k in (3, 2, 1, 0):
        value = a[k][4]
        for j in range(k + 1, 4):
            value = value - a[k][j] * d[j]
        d[k] = value / a[k][k]
    scale = 1.0 / (d[0] + d[1] + d[2] + d[3] + d[4])
    d = [value * scale for value in d]
    c = [None, None, None, d[4]]
    for k in (2, 1, 0):
        c[k] = c[k + 1] + d[k + 1]

    def combine(part):
        x, r = c[0] * part(0), d[0] * part(4)
        for k in range(1, 4):
            x = x + c[k] * part(k)
        for k in range(1, 5):
            r = r + d[k] * part(4 + k)
        return restored(x), restored(r)

    x_mine, r_mine = combine(lambda j: basis[j, pl.ds(s, 1), :])
    swap_copy.wait()
    x_theirs, r_theirs = combine(lambda j: theirs[pl.ds(j, 1), :])
    first = b == 0
    out[pl.ds(0, 1), :] = jnp.where(first, x_mine, x_theirs)
    out[pl.ds(1, 1), :] = jnp.where(first, x_theirs, x_mine)
    out[pl.ds(2, 1), :] = jnp.where(first, r_mine, r_theirs)
    out[pl.ds(3, 1), :] = jnp.where(first, r_theirs, r_mine)
    for copy in sends:
        copy.wait_send()

    @pl.when(sends_across)
    def _():
        for i in range(many):
            across(i).wait_send()


def local(diag_blocks, couplings, cross_weight, right_side):
    nl, ns = lax.axis_size("lines"), lax.axis_size("seg")
    ny = min(4, nl // 2)
    nz, many = nl // (2 * ny), 4 * ny
    shape = jax.ShapeDtypeStruct
    block = pl.BlockSpec(memory_space=pltpu.VMEM)
    vmem, dma = pltpu.VMEM, pltpu.SemaphoreType.DMA
    out = pl.pallas_call(
        functools.partial(kernel, (nl, ns, ny)),
        out_shape=shape((4, 4 * B), F32),
        in_specs=[pl.BlockSpec(memory_space=pltpu.HBM)] * 4,
        out_specs=block,
        scratch_shapes=[
            vmem(diag_blocks.shape, F32),
            vmem(couplings.shape, F32),
            vmem(cross_weight.shape, F32),
            vmem(right_side.shape, F32),
            dma((4,)),
            vmem((8 * B, 2 * B), F32),
            vmem((8 * B, 2 * B), F32),
            vmem((4, 4 * B), F32),
            vmem((ns, B, 2 * B), F32),
            vmem((ns, B, 2 * B), F32),
            vmem((ns, B, 2 * B), F32),
            vmem((ns, B, 2 * B), F32),
            vmem((ns, 4, 4 * B), F32),
            vmem((ns // 2, B, 2 * B), F32),
            vmem((1, 2 * B, 2 * B), F32),
            vmem((ns, 2 * B, 2 * B), F32),
            vmem((ns, B, 2 * B), F32),
            vmem((ns, B, 2 * B), F32),
            vmem((ns, 4 * B, 6 * B), BF16),
            vmem((ns, 4 * B, 6 * B), BF16),
            vmem((8 * B, 4 * B), BF16),
            vmem((8 * B, 4 * B), BF16),
            vmem((ns, 4 * B, 4 * B), BF16),
            vmem((ns, 4 * B, 4 * B), BF16),
            vmem((9, 4, 4 * B), F32),
            vmem((5, 2, 4, 4 * B), F32),
            vmem((4, 4 * B), F32),
            vmem((4, 4 * B), F32),
            vmem((many, 4, 4 * B), F32),
            vmem((8, 4 * B), F32),
            vmem((many, 8, 4 * B), F32),
            vmem((8, 4 * B), F32),
            vmem((16, 4 * B), F32),
            vmem((16, 4 * B), F32),
            vmem((8, 2 * B), F32),
            vmem((nz, 8, 2 * B), F32),
            dma((5, ns)),
            dma((5, ns)),
            dma((5, 2)),
            dma((5, 2)),
            dma((many,)),
            dma((many,)),
            dma((many,)),
            dma((many,)),
            dma((many,)),
            dma((1,)),
            dma((2,)),
            dma((nz,)),
            dma((nz,)),
        ],
        compiler_params=pltpu.CompilerParams(
            collective_id=0, has_side_effects=True
        ),
        name="line_cg",
    )(diag_blocks, couplings, cross_weight, right_side)
    return out[:2], out[2:]


def solution(mesh):
    return jax.shard_map(
        local,
        mesh=mesh,
        in_specs=(
            P("lines", "seg", None),
            P("lines", "seg", None),
            P("lines", "seg"),
            P("lines", "seg"),
        ),
        out_specs=(P("lines", "seg"), P("lines", "seg")),
        check_vma=False,
    )
```

```python
import functools

import jax
import jax.numpy as jnp
from jax import lax
from jax.experimental import pallas as pl
from jax.experimental.pallas import tpu as pltpu
from jax.sharding import PartitionSpec as P

B = 64
F32 = jnp.float32
BF16 = jnp.bfloat16
MESH = pl.DeviceIdType.MESH
EXACT = lax.Precision.HIGHEST


def mm(a, b):
    return jnp.dot(a, b, precision=EXACT, preferred_element_type=F32)


def mm_nt(a, b):
    return lax.dot_general(a, b, (((1,), (1,)), ((), ())), precision=EXACT, preferred_element_type=F32)


def iota(shape, dim):
    return lax.broadcasted_iota(jnp.int32, shape, dim)


def low_lanes(rows):
    return iota((rows, 2 * B), 1) < B


def swap(x):
    return jnp.concatenate([x[:, B:], x[:, :B]], axis=1)


def block_diag(pack):
    low = low_lanes(B)
    return jnp.concatenate([jnp.where(low, pack, 0.0), jnp.where(low, 0.0, pack)], axis=0)


def twice(x):
    return jnp.concatenate([x, x], axis=0)


def permuted(x):
    return jnp.concatenate([x[:, B : 2 * B], x[:, 3 * B :], x[:, 2 * B : 3 * B], x[:, :B]], axis=1)


def restored(x):
    return jnp.concatenate([x[:, 3 * B :], x[:, :B], x[:, 2 * B : 3 * B], x[:, B : 2 * B]], axis=1)


def row_of(x, j):
    return jnp.broadcast_to(x[j : j + 1], x.shape)


def invert(work, packs, beside=iter(()), tiles=1):
    shape = (8, 2 * B)
    wide = 8 * tiles
    size = work.shape[1]
    paired = size == B
    sub, lane = iota(shape, 0), iota(shape, 1)
    low = lane < B
    lane_all = iota((size, 2 * B), 1)
    half = jnp.where(low, 0, B) if paired else jnp.zeros_like(lane)
    half_all = jnp.where(lane_all < B, 0, B) if paired else jnp.zeros_like(lane_all)
    none = jnp.zeros(shape, F32)
    every, each = range(packs), range(tiles)

    def gather(x, at):
        return [jnp.take_along_axis(x, i, axis=1, mode="promise_in_bounds") for i in at]

    def total(terms):
        while len(terms) > 1:
            terms = [x + y for x, y in zip(terms[::2], terms[1::2])]
        return terms[0]

    def cut(x, base):
        return [x[base + 8 * t : base + 8 * t + 8] for t in each]

    whole = [work[p] for p in every]
    rows = [cut(x, 0) for x in whole]
    for q in range(size // wide):
        for _ in each:
            next(beside, None)
        base = wide * q
        within = lane - half - base
        inside = jnp.logical_and(within >= 0, within < wide)
        within_all = lane_all - half_all - base
        inside_all = jnp.logical_and(within_all >= 0, within_all < wide)
        at = [half + base + j for j in range(wide)]
        cols = [[gather(x, at) for x in r] for r in rows]
        more = base + wide < size
        if more:
            after = [cut(x, base + wide) for x in whole]
            after_cols = [[gather(x, at) for x in r] for r in after]
        rows = [[jnp.where(inside, jnp.where(within == sub + 8 * t, 1.0, 0.0), r[t]) for t in each] for r in rows]
        scale = [[none for _ in each] for _ in every]
        for j in range(wide):
            own, at_row = j // 8, j % 8
            mine = sub == at_row
            for p in every:
                g = cols[p]
                inverse = 1.0 / row_of(g[own][j], at_row)
                ratio = [(jnp.where(mine, 0.0, g[t][j]) if t == own else g[t][j]) * inverse for t in each]
                scale[p][own] = jnp.where(mine, inverse, scale[p][own])
                for c in range(j + 1, wide):
                    pivot = row_of(g[own][c], at_row)
                    for t in each:
                        g[t][c] = g[t][c] - ratio[t] * pivot
                pivot = row_of(rows[p][own], at_row)
                rows[p] = [rows[p][t] - ratio[t] * pivot for t in each]
        for p in every:
            new = [rows[p][t] * scale[p][t] for t in each]
            before, behind = [none] * (base // 8), [none] * ((size - base) // 8 - tiles)
            placed = before + new + behind
            if paired:
                left = before + [jnp.where(low, x, 0.0) for x in new] + behind
                placed = left + before + [jnp.where(low, 0.0, x) for x in new] + behind
            weights = jnp.concatenate(placed, axis=0)
            rest = jnp.where(inside_all, 0.0, whole[p]) - mm(jnp.where(inside_all, whole[p], 0.0), weights)
            parts = ([rest[:base]] if q else []) + new + ([rest[base + wide :]] if more else [])
            whole[p] = jnp.concatenate(parts, axis=0)
            if more:
                spread_rows = [row_of(new[j // 8], j % 8) for j in range(wide)]
                rows[p] = [
                    jnp.where(inside, 0.0, after[p][t])
                    - total([x * y for x, y in zip(after_cols[p][t], spread_rows)])
                    for t in each
                ]
    for p in every:
        work[p] = whole[p]


def store_split(high, low, at, value):
    h = value.astype(BF16)
    high[at] = h
    low[at] = (value - h.astype(F32)).astype(BF16)


def apply(row, weights):
    wide = jnp.broadcast_to(row, (16, row.shape[1]))
    high = wide.astype(BF16).astype(F32)
    both = jnp.where(iota(wide.shape, 0) == 0, high, wide - high).astype(BF16)
    out = jnp.dot(jnp.concatenate([both, both], axis=1), weights, preferred_element_type=F32)
    return out[:1] + out[1:2]


def kernel(
    dims, diag_in, coup_in, weight_in, right_in, out, diag, coup, weight, right, in_sem,
    dch, pch, vec, in_d13, in_p10, in_d20, in_p23, in_vec, work, middle, uq_s, et_s, xy_s,
    w1, w2, w3, basis, edge_in, wbuf, wline, plane_w, note, notes, ahead, mine, theirs, sums, sums_in,
    gat_send, gat_recv, edge_send, edge_recv, pw_send, pw_recv, note_send, note_recv, ahead_send, ahead_recv,
    part_sem, sum_send, sum_recv,
):
    nl, ns, ny = dims
    w1h, w1l = w1.at[:, : 4 * B, :], w1.at[:, 4 * B :, :]
    w2h, w2l = w2.at[: 8 * B, :], w2.at[8 * B :, :]
    w3h, w3l = w3.at[:, : 4 * B, :], w3.at[:, 4 * B :, :]
    m, s = lax.axis_index("lines"), lax.axis_index("seg")
    core, y_at, z_at = lax.rem(m, 2), lax.rem(m // 2, ny), m // (2 * ny)
    nz = nl // (2 * ny)

    def line_of(seg):
        return lax.rem(lax.rem((seg + 1) // 2, 2) + m, 2)

    b = line_of(s)
    mate = s + 1 - 2 * lax.rem(s, 2)
    partner = (m, mate)
    other = (lax.rem(m - 1 + 2 * b + nl, nl), s)
    others = [lax.rem(s + d, ns) for d in range(1, ns)]

    def near(index):
        at, turned = index // 2, lax.rem(index + index // 2, 2)
        return (z_at * ny * 2 + at, (s // 2) * (3 - 2 * turned) + turned)

    def far(index):
        return ((index * ny + y_at) * 2 + core, s)

    groups = ((near, 4 * ny, (y_at * 2 + core) * 2 + b), (far, nz, z_at))
    many, rank = groups[0][1:]
    step = 2 * ny

    def shifted(place, by):
        return (lax.rem(place[0] + by + nl, nl), place[1])

    herald = shifted(near(0), step)
    sends_across = rank == 0
    peers = [(m, x) for x in others]
    for place, size, own in groups[::-1]:
        away = sorted(range(1, size), key=lambda d: -min(d, size - d))
        peers += [place(lax.rem(own + d, size)) for d in away]
    peers += [other, herald]
    pairs = ((diag_in, diag), (coup_in, coup), (weight_in, weight), (right_in, right))
    loads = [pltpu.make_async_copy(src, dst, in_sem.at[i]) for i, (src, dst) in enumerate(pairs)]
    barrier = pltpu.get_barrier_semaphore()
    for peer in peers:
        pl.semaphore_signal(barrier, inc=1, device_id=peer, device_id_type=MESH)

    for load in loads:
        load.start()

    @pl.when(sends_across)
    def _():
        for i in range(many):
            pl.semaphore_signal(barrier, inc=1, device_id=shifted(near(i), -step), device_id_type=MESH)

    not_first = iota((4, 2 * B), 0) > 0
    low4 = low_lanes(4)

    def lay_out(dst, tile_of, order):
        for l in range(2):
            for k in range(B // 2):
                x = tile_of(l, pl.ds(2 * B * k, 2 * B))
                xt = swap(x)
                mate_x = jnp.concatenate([x[i : i + 1] for i in order], axis=0)
                mate_t = jnp.concatenate([xt[i : i + 1] for i in order], axis=0)
                dst[pl.ds(4 * B * l + 2 * k, 4, stride=B), :] = jnp.where(low4, x, mate_t)
                dst[pl.ds(4 * B * l + 2 * k + 1, 4, stride=B), :] = jnp.where(low4, xt, mate_x)

    def diagonal(l, cols):
        edge = coup[l, :, cols]
        before = jnp.concatenate([edge[3:], edge[:3]], axis=0)
        return diag[l, :, cols] + edge + jnp.where(not_first, before, 0.0)

    loads[0].wait()
    loads[1].wait()
    lay_out(dch, diagonal, (2, 3, 0, 1))
    pl.semaphore_wait(barrier, len(peers) + jnp.where(sends_across, many, 0))

    sends = []

    def drain(keep):
        gone = sends[: len(sends) - keep]
        del sends[: len(gone)]
        for copy in gone:
            copy.wait_send()

    chunks = ((dch, 1, in_d13), (pch, 1, in_p10), (dch, 2, in_d20), (pch, 2, in_p23))

    def chunk_copy(i, to, slot, d):
        if i == len(chunks):
            src, dst = vec, in_vec
        else:
            array, e, dst = chunks[i]
            src = array.at[pl.ds(pl.multiple_of(4 * B * line_of(to) + B * e, B), B), :]
        return pltpu.make_async_remote_copy(
            src_ref=src,
            dst_ref=dst.at[slot],
            send_sem=gat_send.at[i, d],
            recv_sem=gat_recv.at[i, slot],
            device_id=(m, to),
            device_id_type=MESH,
        )

    def send_chunk(i):
        for d, to in enumerate(others):
            copy = chunk_copy(i, to, s, d)
            copy.start()
            sends.append(copy)

    send_chunk(0)
    lay_out(pch, lambda l, cols: coup[l, :, cols], (1, 0, 3, 2))
    send_chunk(1)
    send_chunk(3)
    loads[2].wait()
    loads[3].wait()
    vec[...] = jnp.concatenate([permuted(right[...]), permuted(weight[...])], axis=0)
    send_chunk(4)
    send_chunk(2)

    def arrived(i):
        if i == len(chunks):
            in_vec[s] = vec[...]
        else:
            array, e, dst = chunks[i]
            dst[s] = array[pl.ds(pl.multiple_of(4 * B * b + B * e, B), B), :]
        for d, origin in enumerate(others):
            chunk_copy(i, origin, origin, d).wait_recv()

    def exchange(turn, source, targets):
        copies = []
        for side, to in targets:
            copy = pltpu.make_async_remote_copy(
                src_ref=source,
                dst_ref=edge_in.at[turn, side],
                send_sem=edge_send.at[turn, side],
                recv_sem=edge_recv.at[turn, side],
                device_id=to,
                device_id_type=MESH,
            )
            copy.start()
            copies.append(copy)
            sends.append(copy)

        def finish():
            for copy in copies:
                copy.wait_recv()

        return finish

    def spread(place, size, own, source, inbox, send_sem, recv_sem):
        for d in sorted(range(1, size), key=lambda d: -min(d, size - d)):
            copy = pltpu.make_async_remote_copy(
                src_ref=source,
                dst_ref=inbox.at[own],
                send_sem=send_sem.at[d],
                recv_sem=recv_sem.at[own],
                device_id=place(lax.rem(own + d, size)),
                device_id_type=MESH,
            )
            copy.start()
            sends.append(copy)
        inbox[own] = source[...]

        def finish():
            for d in range(1, size):
                origin = lax.rem(own + d, size)
                pltpu.make_async_remote_copy(
                    src_ref=source,
                    dst_ref=inbox.at[origin],
                    send_sem=send_sem.at[d],
                    recv_sem=recv_sem.at[origin],
                    device_id=place(origin),
                    device_id_type=MESH,
                ).wait_recv()

        return finish

    low = low_lanes(B)
    runs = range(ns)
    arrived(0)
    invert(in_d13, ns)
    arrived(1)
    arrived(3)
    for r in runs:
        p10, p23 = in_p10[r], in_p23[r]
        if r == ns - 1:
            p23 = jnp.where(low, p23, 0.0)
        uq = mm(block_diag(in_d13[r]), jnp.concatenate([p10, p23], axis=0))
        uq_s[r] = uq
        a1 = mm(block_diag(p10), twice(uq[:B]))
        a3 = mm(block_diag(p23), twice(uq[B:]))
        if r == 0:
            arrived(2)
        d20 = in_d20[r]
        s2 = d20 - a1[:B] - a3[:B]
        if r % 2 == 0:
            work[r // 2] = s2
        else:
            work[r // 2] = jnp.where(low, work[r // 2], swap(s2))
        et_s[r] = jnp.where(low, swap(a3[:B]), a1[:B])
        xy_s[r] = jnp.where(low, swap(p23 - a3[B:]), d20 - a1[B:])
    arrived(4)
    w_mate = jnp.concatenate([in_vec[r, pl.ds(2, 1), :] for r in runs], axis=0)
    w_own = jnp.concatenate([in_vec[r, pl.ds(3, 1), :] for r in runs], axis=0)
    wbuf[...] = w_own
    wait_weights = exchange(4, wbuf, ((1, other),))
    invert(work, ns // 2, tiles=2)
    zs, zts, ss, fts, i2s = [], [], [], [], []
    eye = jnp.where(iota((B, 2 * B), 0) + B == iota((B, 2 * B), 1), 1.0, 0.0)
    for r in runs:
        pack = work[r // 2]
        i2 = (pack if r % 2 == 0 else swap(pack))[:, :B]
        et = et_s[r]
        ft = mm(i2, et)
        cross = mm(et.T, ft)
        xy = xy_s[r] - jnp.where(low, cross[:B], cross[B:])
        zs.append(cross[B:, :B])
        zts.append(cross[:B, B:])
        ss.append(xy)
        fts.append(ft)
        i2s.append(i2)

    t = jnp.concatenate([in_vec[r, pl.ds(b, 1), :] for r in runs], axis=0)
    begun = []

    def operators():
        for r in runs:
            uq = uq_s[r]
            ui = jnp.concatenate([uq[:, :B], eye[:, B:]], axis=0)
            t1 = mm(ui, jnp.concatenate([fts[r], i2s[r]], axis=1))
            yield
            q0 = jnp.where(low, 0.0, uq[:B])
            q3 = jnp.where(low, swap(uq[B:]), 0.0)
            h = t1[:, : 2 * B] + jnp.concatenate([q0, q3, jnp.zeros((B, 2 * B), F32)], axis=0)
            h = jnp.concatenate([h, eye], axis=0)
            store_split(w1h, w1l, (r, slice(None), slice(4 * B, 6 * B)), h)
            yield
            t2 = mm_nt(t1[:, 2 * B :], ui)
            g = t2[: 2 * B, : 2 * B] + block_diag(in_d13[r])
            g = jnp.concatenate([g, t2[2 * B :, : 2 * B], jnp.zeros((B, 2 * B), F32)], axis=0)
            store_split(w1h, w1l, (r, slice(None), slice(0, 2 * B)), g)
            yield
            g = jnp.concatenate([t2[:, 2 * B :], jnp.zeros((B, B), F32)], axis=0)
            g = jnp.concatenate([g, jnp.zeros((4 * B, B), F32)], axis=1)
            store_split(w1h, w1l, (r, slice(None), slice(2 * B, 4 * B)), g)
            yield
            ht = h.T
            w3h[r] = jnp.zeros((4 * B, 4 * B), BF16)
            w3l[r] = jnp.zeros((4 * B, 4 * B), BF16)
            store_split(w3h, w3l, (r, slice(B * r, B * r + B)), ht[B:])
            if r < ns - 1:
                store_split(w3h, w3l, (r, slice(B * r + B, B * r + 2 * B)), ht[:B])
            yield
            begun.append(apply(t[r : r + 1], w1[r]))
            yield

    beside = operators()

    def separator(r):
        own = ss[r][:, B:]
        return own if r == 0 else own + ss[r - 1][:, :B]

    s0, s1, s2, s3 = (separator(r) for r in runs)
    work[0] = jnp.concatenate([s0, s3], axis=1)
    invert(work, 1, beside, 2)
    j0, j3 = work[0, :, :B], work[0, :, B:]
    v0, v3 = mm(j0, zs[0]), mm(j3, zts[2])
    s1 = s1 - mm(zts[0], v0)
    s2 = s2 - mm(zs[2], v3)
    middle[0, :B, :] = jnp.concatenate([s1, -zs[1]], axis=1)
    middle[0, B:, :] = jnp.concatenate([-zts[1], s2], axis=1)
    invert(middle, 1, beside, 2)
    for _ in beside:
        pass
    inner = middle[0]
    zero = jnp.zeros((B, B), F32)
    v = jnp.concatenate([jnp.concatenate([v0, zero], axis=1), jnp.concatenate([zero, v3], axis=1)], axis=0)
    side = mm(v, inner)
    corner = mm_nt(side, v)
    back = mm_nt(inner, v)
    rows = (
        jnp.concatenate([j0 + corner[:B, :B], side[:B], corner[:B, B:]], axis=1),
        jnp.concatenate([back[:B, :B], inner[:B], back[:B, B:]], axis=1),
        jnp.concatenate([back[B:, :B], inner[B:], back[B:, B:]], axis=1),
        jnp.concatenate([corner[B:, :B], side[B:], j3 + corner[B:, B:]], axis=1),
    )
    for r in runs:
        after = rows[r + 1] if r + 1 < ns else jnp.zeros((B, 4 * B), F32)
        store_split(w2h, w2l, (slice(2 * B * r, 2 * B * r + B),), after)
        store_split(w2h, w2l, (slice(2 * B * r + B, 2 * B * r + 2 * B),), rows[r])

    def begin(t):
        return [apply(t[r : r + 1], w1[r]) for r in runs]

    def solve(first):
        f = jnp.concatenate([x[:, 4 * B :] for x in first], axis=1)
        u = apply(f, w2[...])
        out = [first[r][:, : 4 * B] + apply(u, w3[r]) for r in runs]
        return jnp.concatenate(out, axis=0)

    def folded(x):
        x = jnp.sum(x, axis=0, keepdims=True)
        return x[:, : 2 * B] + x[:, 2 * B :]

    def moment(i):
        note[4 + i // 2 : 5 + i // 2, 2 * B * (i % 2) : 2 * B * (i % 2) + 2 * B] = folded(
            ys[i // 2] * ts[(i + 1) // 2]
        )

    note[7:8, 2 * B :] = jnp.zeros((1, 2 * B), F32)
    ts, ys = [t], []
    basis[4] = t
    for turn in range(4):
        ys.append(solve(begin(ts[turn]) if turn else begun))
        basis[turn] = ys[turn]
        if turn == 3:
            break
        arrive = exchange(turn, basis.at[turn], ((0, partner), (1, other)))
        drain(2)
        if turn == 0:
            wline[...] = jnp.where(b == 0, w_mate, w_own)
            wait_plane = spread(near, many, rank, wline, plane_w, pw_send, pw_recv)
            wait_weights()
            w_other = jnp.where(b == 0, edge_in[4, 1], w_own)
        moment(2 * turn)
        if turn:
            moment(2 * turn - 1)
        arrive()
        ts.append(w_mate * edge_in[turn, 0] + w_other * edge_in[turn, 1])
        basis[5 + turn] = ts[turn + 1]

    note[0:4, :] = ys[3]
    moment(5)
    moment(6)
    def across(to):
        return pltpu.make_async_remote_copy(
            src_ref=note.at[...],
            dst_ref=ahead,
            send_sem=ahead_send.at[to],
            recv_sem=ahead_recv.at[0],
            device_id=shifted(near(to), -step),
            device_id_type=MESH,
        )

    @pl.when(sends_across)
    def _():
        for i in sorted(range(many), key=lambda i: -min(i, many - i)):
            across(i).start()

    wait_notes = spread(near, many, rank, note, notes, note_send, note_recv)
    arrive = exchange(3, basis.at[3], ((0, partner), (1, other)))
    drain(many + 1)
    wait_plane()
    wait_notes()
    pltpu.make_async_remote_copy(
        src_ref=note.at[...],
        dst_ref=ahead,
        send_sem=ahead_send.at[0],
        recv_sem=ahead_recv.at[0],
        device_id=herald,
        device_id_type=MESH,
    ).wait_recv()
    last = jnp.zeros((ns, 4 * B), F32)
    total = jnp.zeros((ns, 4 * B), F32)
    for i in range(many):
        following = notes[i + 1, 0:4, :] if i + 1 < many else ahead[0:4, :]
        last = last + plane_w[i] * notes[i, 0:4, :] * following
        total = total + notes[i, 4:8, :]
    last = 2.0 * folded(last)
    for i in range(8):
        sums[pl.ds(i, 1), :] = last if i == 7 else total[i // 2 : i // 2 + 1, 2 * B * (i % 2) : 2 * B * (i % 2) + 2 * B]
    wait_sums = spread(far, nz, z_at, sums, sums_in, sum_send, sum_recv)
    arrive()
    ts.append(w_mate * edge_in[3, 0] + w_other * edge_in[3, 1])
    basis[8] = ts[4]
    for j in range(9):
        mine[pl.ds(j, 1), :] = basis[j, pl.ds(mate, 1), :]
    swap_copy = pltpu.make_async_remote_copy(
        src_ref=mine,
        dst_ref=theirs,
        send_sem=part_sem.at[0],
        recv_sem=part_sem.at[1],
        device_id=partner,
        device_id_type=MESH,
    )
    swap_copy.start()
    drain(nz - 1)

    @pl.when(sends_across)
    def _():
        for i in range(many):
            across(i).wait_send()

    wait_sums()
    total = sums_in[0]
    for i in range(1, nz):
        total = total + sums_in[i]
    total = jnp.sum(total, axis=1, keepdims=True)
    moments = [total[i : i + 1] for i in range(8)]
    a = [[moments[i + j] for j in range(4)] + [-moments[i + 4]] for i in range(4)]
    for k in range(3):
        inverse = 1.0 / a[k][k]
        for i in range(k + 1, 4):
            ratio = a[i][k] * inverse
            for j in range(k + 1, 5):
                a[i][j] = a[i][j] - ratio * a[k][j]
    d = [None] * 4 + [jnp.ones((1, 1), F32)]
    for k in (3, 2, 1, 0):
        value = a[k][4]
        for j in range(k + 1, 4):
            value = value - a[k][j] * d[j]
        d[k] = value / a[k][k]
    scale = 1.0 / (d[0] + d[1] + d[2] + d[3] + d[4])
    d = [value * scale for value in d]
    c = [None, None, None, d[4]]
    for k in (2, 1, 0):
        c[k] = c[k + 1] + d[k + 1]

    def combine(part):
        x, r = c[0] * part(0), d[0] * part(4)
        for k in range(1, 4):
            x = x + c[k] * part(k)
        for k in range(1, 5):
            r = r + d[k] * part(4 + k)
        return restored(x), restored(r)

    x_mine, r_mine = combine(lambda j: basis[j, pl.ds(s, 1), :])
    swap_copy.wait()
    x_theirs, r_theirs = combine(lambda j: theirs[pl.ds(j, 1), :])
    first = b == 0
    out[pl.ds(0, 1), :] = jnp.where(first, x_mine, x_theirs)
    out[pl.ds(1, 1), :] = jnp.where(first, x_theirs, x_mine)
    out[pl.ds(2, 1), :] = jnp.where(first, r_mine, r_theirs)
    out[pl.ds(3, 1), :] = jnp.where(first, r_theirs, r_mine)
    drain(0)


def local(diag_blocks, couplings, cross_weight, right_side):
    nl, ns = lax.axis_size("lines"), lax.axis_size("seg")
    ny = min(4, nl // 2)
    nz, many = nl // (2 * ny), 4 * ny
    shape = jax.ShapeDtypeStruct
    block = pl.BlockSpec(memory_space=pltpu.VMEM)
    vmem, dma = pltpu.VMEM, pltpu.SemaphoreType.DMA
    out = pl.pallas_call(
        functools.partial(kernel, (nl, ns, ny)),
        out_shape=shape((4, 4 * B), F32),
        in_specs=[pl.BlockSpec(memory_space=pltpu.HBM)] * 4,
        out_specs=block,
        scratch_shapes=[
            vmem(diag_blocks.shape, F32),
            vmem(couplings.shape, F32),
            vmem(cross_weight.shape, F32),
            vmem(right_side.shape, F32),
            dma((4,)),
            vmem((8 * B, 2 * B), F32),
            vmem((8 * B, 2 * B), F32),
            vmem((4, 4 * B), F32),
            vmem((ns, B, 2 * B), F32),
            vmem((ns, B, 2 * B), F32),
            vmem((ns, B, 2 * B), F32),
            vmem((ns, B, 2 * B), F32),
            vmem((ns, 4, 4 * B), F32),
            vmem((ns // 2, B, 2 * B), F32),
            vmem((1, 2 * B, 2 * B), F32),
            vmem((ns, 2 * B, 2 * B), F32),
            vmem((ns, B, 2 * B), F32),
            vmem((ns, B, 2 * B), F32),
            vmem((ns, 8 * B, 6 * B), BF16),
            vmem((16 * B, 4 * B), BF16),
            vmem((ns, 8 * B, 4 * B), BF16),
            vmem((9, 4, 4 * B), F32),
            vmem((5, 2, 4, 4 * B), F32),
            vmem((4, 4 * B), F32),
            vmem((4, 4 * B), F32),
            vmem((many, 4, 4 * B), F32),
            vmem((8, 4 * B), F32),
            vmem((many, 8, 4 * B), F32),
            vmem((8, 4 * B), F32),
            vmem((16, 4 * B), F32),
            vmem((16, 4 * B), F32),
            vmem((8, 2 * B), F32),
            vmem((nz, 8, 2 * B), F32),
            dma((5, ns)),
            dma((5, ns)),
            dma((5, 2)),
            dma((5, 2)),
            dma((many,)),
            dma((many,)),
            dma((many,)),
            dma((many,)),
            dma((many,)),
            dma((1,)),
            dma((2,)),
            dma((nz,)),
            dma((nz,)),
        ],
        compiler_params=pltpu.CompilerParams(
            collective_id=0, has_side_effects=True
        ),
        name="line_cg",
    )(diag_blocks, couplings, cross_weight, right_side)
    return out[:2], out[2:]


def solution(mesh):
    return jax.shard_map(
        local,
        mesh=mesh,
        in_specs=(
            P("lines", "seg", None),
            P("lines", "seg", None),
            P("lines", "seg"),
            P("lines", "seg"),
        ),
        out_specs=(P("lines", "seg"), P("lines", "seg")),
        check_vma=False,
    )
```
